256 devices in a mesh: group: 2 (over y_lo), expert: 16 (over z, core), shard: 8 (over x, y_hi).
Axes of the slice: x: 4, y: 4 (y_hi: 2, y_lo: 2; y = y_hi * 2 + y_lo), z: 8, core: 2. Of those that a mesh axis runs over, the one named last changes fastest.
Arguments:
- hidden: bfloat16 [2560, 6144], P(('group', 'expert', 'shard')), may hold values from -6 to 6
- expert_ids: int32 [2560, 2], P(('group', 'expert', 'shard')), may hold values from 0 to 7, all different within a row; in each aligned block of 10 rows (0 to 9, 10 to 19, ...) at most 3 rows name the same one
- gate_logits: float32 [2560, 2], P(('group', 'expert', 'shard')), may hold values from -6 to 6
- accept_len: int32 [512], P(('group', 'expert', 'shard')), may hold values from 0 to 4
- w_gate: bfloat16 [6144, 65536], P(None, ('group', 'expert', 'shard')), may hold values from -0.078125 to 0.078125
- w_up: bfloat16 [6144, 65536], P(None, ('group', 'expert', 'shard')), may hold values from -0.078125 to 0.078125
- w_down: bfloat16 [65536, 6144], P(('group', 'expert', 'shard')), may hold values from -0.0625 to 0.0625
- draft_in: bfloat16 [6144, 896], P(None, ('group', 'shard')), may hold values from -0.078125 to 0.078125
- draft_out: bfloat16 [896, 6144], P(('group', 'shard')), may hold values from -0.1875 to 0.1875
Outputs:
- verified: bfloat16 [2560, 6144], P(('group', 'expert', 'shard'))
- new_in: bfloat16 [6144, 896], P(None, ('group', 'shard'))
- new_out: bfloat16 [896, 6144], P(('group', 'shard'))
The draws below stay inside these ranges and needn't reach their ends.
Inputs may be any that keep to these rules, and one draw needn't show every extreme that they name: `expert_ids`: the two experts of a row differ. Among the 10 rows of one device no expert is named more than 3 times, and every draw has an expert named exactly 3 times by one device's rows. `accept_len`: every request rejects at least its last position.
All inputs are finite; a program needn't handle non-finite values.
Results may differ from the reference program's by a relative error of at most 0.014.
Values may be sent and summed in bfloat16 or wider, within the bound.
No kernel may reach another device: no remote copies, remote signals or barrier semaphores. Data moves between devices by JAX's collectives and lax.ppermute only.
A program may use at most 128 MiB of HBM per device.

```python
import math
import jax
import jax.numpy as jnp
import numpy as np
from jax import lax

D = 6144
FF = 8192
EXPERTS = 8
DR = 896
DRAFT = 5
TOK_DEV = 10
CAP = 3
REQUESTS = 512
TOKENS = 2560
N_GROUP = 2
N_EXPERT = 16
N_SHARD = 8


def plant(result, rng, least, high):
    longest = result.shape.index(max(result.shape))
    spots = []
    for shift in (0, 1):
        where = [jax.random.randint(jax.random.fold_in(rng, axis), (), 0, length) for axis, length in enumerate(result.shape)]
        where[longest] = (where[longest] + shift) % result.shape[longest]
        spots.append(tuple(where))
    return result.at[spots[0]].set(least).at[spots[1]].set(high)


def block_levels(stream_key, extent, pieces, smallest, top_value):
    loudness = 1.0
    for axis_at, blocks in pieces:
        steps = jax.random.uniform(jax.random.fold_in(jax.random.fold_in(stream_key, 6), axis_at), (blocks,), jnp.float32, smallest / len(pieces), top_value / len(pieces))
        loudness = loudness * jnp.repeat(jnp.exp(steps), extent[axis_at] // blocks).reshape((-1,) + (1,) * (len(extent) - 1 - axis_at))
    return loudness


def shared_out(rng, own, number, rows, number_of, top, reach, lean):
    ranking = jax.random.permutation(rng, number_of)
    packed, ordinary = load_shares(number_of, rows * top, reach, lean, True), load_shares(number_of, rows * top, reach, lean, False)
    places = jnp.arange(number_of)

    def named(sizes, rotation):
        used = int((sizes > 0).sum())
        fixed = max(1, used // 4)
        moved = fixed + (places - fixed + rotation * (used - fixed)) % max(1, number_of - fixed)
        return jnp.zeros((number_of,), jnp.int32).at[ranking[jnp.where(places < fixed, places, moved)]].set(jnp.asarray(sizes, jnp.int32))

    sizes = jnp.where(number % 4 == 0, named(packed, number // 4), named(ordinary, number - number // 4 - 1))
    mixed = jax.random.permutation(jax.random.fold_in(own, 3), number_of)
    source_of, taker = mixed[0:number_of // 2 * 2:2], mixed[1:number_of // 2 * 2:2]
    slack = jnp.minimum(sizes[source_of] - 1, reach - sizes[taker]) // 2
    slack = jnp.where((source_of == ranking[0]) | (taker == ranking[0]) | (sizes[taker] == 0), 0, jnp.maximum(slack, 0))
    moved = jax.random.randint(jax.random.fold_in(own, 4), (number_of // 2,), 0, 1 << 20) % (slack + 1)
    sizes = sizes.at[source_of].add(-moved).at[taker].add(moved)
    labels = jnp.searchsorted(jnp.cumsum(sizes), jnp.arange(rows * top), side="right").astype(jnp.int32)
    grid = labels.reshape(top, rows).T
    grid = grid[jax.random.permutation(jax.random.fold_in(own, 1), rows)]
    rotation = jax.random.randint(jax.random.fold_in(own, 2), (rows, 1), 0, top)
    return jnp.take_along_axis(grid, (jnp.arange(top)[None, :] + rotation) % top, axis=1)


def load_shares(number_of, total, limit, lean, full):
    portions = [(1 << 20) // math.isqrt(standing ** lean) + 1 for standing in range(1, number_of + 1)]
    largest = limit if full else min(limit, max(-(-total // number_of), total * portions[0] // sum(portions)))
    least = 1 if total - largest >= number_of - 1 else 0
    counts, spare = [largest] + [least] * (number_of - 1), total - largest - least * (number_of - 1)
    while spare > 0:
        candidates = [i for i in range(1, number_of) if counts[i] < largest] or [i for i in range(1, number_of) if counts[i] < limit]
        whole, left = sum([portions[i] for i in candidates]), spare
        for i in candidates:
            extra = min(limit - counts[i], max(1, left * portions[i] // whole), spare)
            counts[i] = counts[i] + extra
            spare = spare - extra
    return np.array(counts)


def centred(rng, dims, scale, most, split=(), held_as=jnp.bfloat16):
    values = jax.random.normal(rng, dims, jnp.float32) * scale
    if len(split) > 0:
        values = block_levels(rng, dims, split, -0.22, 0.18) * values
    return jnp.clip(values, min=-most, max=most).astype(held_as)


def setup_inputs(seed: int = 0) -> dict:
    seeds = jax.random.split(jax.random.key(seed), 10)
    hidden = centred(seeds[0], (TOKENS, D), 1.0, 6.0, ((0, 256),))
    expert_ids_keys = jax.random.split(jax.random.fold_in(seeds[1], 1), TOKENS // TOK_DEV)
    expert_ids_turns = jax.random.permutation(jax.random.fold_in(seeds[1], 3), TOKENS // TOK_DEV)
    expert_ids = jax.vmap(lambda own, number: shared_out(jax.random.fold_in(seeds[1], 2), own, number, TOK_DEV, EXPERTS, 2, CAP, 2))(expert_ids_keys, expert_ids_turns).reshape((TOKENS, 2))
    gate_logits = centred(seeds[2], (TOKENS, 2), 1.5, 6.0, ((0, 256),), jnp.float32)
    accept_len = plant(jax.random.randint(seeds[3], (REQUESTS,), 0, DRAFT), jax.random.fold_in(seeds[3], 1), 0, DRAFT - 1).astype(jnp.int32)
    w_gate = centred(seeds[4], (D, EXPERTS * FF), D ** -0.5, 0.078125, ((1, 256),))
    w_up = centred(seeds[5], (D, EXPERTS * FF), D ** -0.5, 0.078125, ((1, 256),))
    w_down = centred(seeds[6], (EXPERTS * FF, D), FF ** -0.5, 0.0625, ((0, 256),))
    draft_in = centred(seeds[7], (D, DR), D ** -0.5, 0.078125, ((1, 16),))
    draft_out = centred(seeds[8], (DR, D), DR ** -0.5, 0.1875, ((0, 16),))
    return dict(hidden=hidden, expert_ids=expert_ids, gate_logits=gate_logits, accept_len=accept_len, w_gate=w_gate, w_up=w_up, w_down=w_down, draft_in=draft_in, draft_out=draft_out)


LEARNING_RATE = 0.5


def slot_places(expert_ids, devices):
    pairs = expert_ids.reshape(devices, TOK_DEV * 2)
    onehot = (pairs[:, :, None] == jnp.arange(EXPERTS, dtype=jnp.int32)[None, None, :]).astype(jnp.int32)
    before = jnp.cumsum(onehot, axis=1) - onehot
    slot_index = jnp.sum(before * onehot, axis=2)
    source = jnp.broadcast_to(jnp.arange(devices, dtype=jnp.int32)[:, None], pairs.shape)
    places = (pairs * devices + source) * CAP + slot_index
    return places.reshape(-1).astype(jnp.int32)


def reference(hidden, expert_ids, gate_logits, accept_len, w_gate, w_up, w_down, draft_in, draft_out):
    devices = N_GROUP * N_EXPERT * N_SHARD
    quarters = N_GROUP * N_EXPERT // EXPERTS
    width = FF // (quarters * N_SHARD)
    places = slot_places(expert_ids, devices)
    token_of = (jnp.arange(TOKENS * 2, dtype=jnp.int32) // 2).astype(jnp.int32)
    slots = EXPERTS * devices * CAP
    index_of = jnp.full((slots,), TOKENS, dtype=jnp.int32).at[places].set(token_of)
    padded = jnp.concatenate([hidden, jnp.zeros((1, D), hidden.dtype)], axis=0)
    routed = padded[index_of].reshape(EXPERTS, devices * CAP, D)

    def one_expert(operands):
        block, expert = operands
        start = (expert * FF).astype(jnp.int32)
        gate = jnp.dot(block, lax.dynamic_slice_in_dim(w_gate, start, FF, 1), preferred_element_type=jnp.float32)
        upper = jnp.dot(block, lax.dynamic_slice_in_dim(w_up, start, FF, 1), preferred_element_type=jnp.float32)
        active = (jax.nn.silu(gate) * upper).astype(jnp.bfloat16)
        down = lax.dynamic_slice_in_dim(w_down, start, FF, 0)
        total = jnp.zeros((devices * CAP, D), jnp.float32)
        for quarter in range(quarters):
            partial_sum = jnp.zeros((devices * CAP, D), jnp.float32)
            for piece in range(N_SHARD):
                first = (quarter * N_SHARD + piece) * width
                term = jnp.dot(active[:, first:first + width], down[first:first + width], preferred_element_type=jnp.float32)
                partial_sum = partial_sum + lax.optimization_barrier(term.astype(jnp.bfloat16)).astype(jnp.float32)
            total = total + lax.optimization_barrier(partial_sum.astype(jnp.bfloat16)).astype(jnp.float32)
        return total

    results = lax.map(one_expert, (routed, jnp.arange(EXPERTS, dtype=jnp.int32)))
    values = results.reshape(slots, D)[places].reshape(TOKENS, 2, D)
    first_gate = 1.0 / (1.0 + jnp.exp(gate_logits[:, 1] - gate_logits[:, 0]))
    second_gate = 1.0 / (1.0 + jnp.exp(gate_logits[:, 0] - gate_logits[:, 1]))
    combined = first_gate[:, None] * values[:, 0] + second_gate[:, None] * values[:, 1]
    verified = (hidden.astype(jnp.float32) + combined).astype(jnp.bfloat16)
    target = combined.astype(jnp.bfloat16)

    keep = jnp.arange(TOKENS, dtype=jnp.int32) % DRAFT >= jnp.repeat(accept_len, DRAFT)
    student_in = jnp.where(keep[:, None], hidden, jnp.zeros_like(hidden))
    teacher = jnp.where(keep[:, None], target, jnp.zeros_like(target))
    rejected = jnp.sum(DRAFT - accept_len).astype(jnp.float32)
    inner = jnp.dot(student_in, draft_in, preferred_element_type=jnp.float32)
    active_rows = jax.nn.silu(inner).astype(jnp.bfloat16)
    guess = jnp.dot(active_rows, draft_out, preferred_element_type=jnp.float32)
    slope = (2.0 * (guess - teacher.astype(jnp.float32)) / rejected).astype(jnp.bfloat16)
    grad_out = jnp.dot(active_rows.T, slope, preferred_element_type=jnp.float32)
    back_inner = jnp.dot(slope, draft_out.T, preferred_element_type=jnp.float32)
    sigma = jax.nn.sigmoid(inner)
    delta = (back_inner * sigma * (1.0 + inner * (1.0 - sigma))).astype(jnp.bfloat16)
    grad_in = jnp.dot(student_in.T, delta, preferred_element_type=jnp.float32)
    new_in = (draft_in.astype(jnp.float32) - LEARNING_RATE * grad_in).astype(jnp.bfloat16)
    new_out = (draft_out.astype(jnp.float32) - LEARNING_RATE * grad_out).astype(jnp.bfloat16)
    return (verified, new_in, new_out)
```

```python
import itertools

import jax
import jax.numpy as jnp
from jax import lax
from jax.sharding import PartitionSpec as P

EXPERTS = 8
DRAFT = 5
CAP = 3
LEARNING_RATE = 0.5
AXES = ("group", "expert", "shard")
PARTS = (2, 8, 2, 4, 2)


def flat(place):
    index = 0
    for size, at in zip(PARTS, place):
        index = index * size + at
    return index


def permute(value, move):
    pairs = []
    for place in itertools.product(*(range(size) for size in PARTS)):
        pairs.append((flat(place), flat(move(*place))))
    return lax.ppermute(value, AXES, pairs)


def other_core(g, z, c, x, h):
    return g, z, 1 - c, x, h


def x_step(by):
    return lambda g, z, c, x, h: (g, z, c, (x + by) % 4, h)


def y_step(by):
    def move(g, z, c, x, h):
        y = (2 * h + g + by) % 4
        return y % 2, z, c, x, y // 2

    return move


def z_step(by):
    return lambda g, z, c, x, h: (g, (z + by) % 8, c, x, h)


def z_swap(g, z, c, x, h):
    return g, z ^ 1, c, x, h


def h_swap(g, z, c, x, h):
    return g, z, c, x, 1 - h


def by_core(first, second):
    return lambda g, z, c, x, h: (second if c else first)(g, z, c, x, h)


X_RING = (x_step(1), x_step(-1), x_step(1), x_step(-1))
X_BACK = (x_step(-1), x_step(1), x_step(-1), x_step(1))
Y_RING = (y_step(1), y_step(-1), y_step(1), y_step(-1))
Y_BACK = (y_step(-1), y_step(1), y_step(-1), y_step(1))
SQUARE = (z_swap, h_swap, h_swap, z_swap)


def mixed(first, second):
    return tuple(by_core(a, b) for a, b in zip(first, second))


BLOCK_RINGS = (mixed(SQUARE, X_RING), mixed(X_RING, SQUARE))
BLOCK_BACK = (mixed(SQUARE, X_BACK), mixed(X_BACK, SQUARE))
PLANE_RINGS = (mixed(X_RING, Y_RING), mixed(Y_RING, X_RING))
PLANE_BACK = (mixed(X_BACK, Y_BACK), mixed(Y_BACK, X_BACK))


def ring_gather(value, ring):
    half = value.shape[1] // 2
    a = permute(value, ring[0])
    b = permute(value, ring[1])
    far_left = permute(a[:, :half], ring[2])
    far_right = permute(b[:, half:], ring[3])
    return a, b, far_left, far_right


def ring_reduce(own, a, b, far_left, far_right, back):
    half = own.shape[1] // 2
    far_left = permute(far_left.astype(jnp.bfloat16), back[2]).astype(jnp.float32)
    far_right = permute(far_right.astype(jnp.bfloat16), back[3]).astype(jnp.float32)
    a = jnp.concatenate([a[:, :half] + far_left, a[:, half:]], axis=1)
    b = jnp.concatenate([b[:, :half], b[:, half:] + far_right], axis=1)
    a = permute(a.astype(jnp.bfloat16), back[0]).astype(jnp.float32)
    b = permute(b.astype(jnp.bfloat16), back[1]).astype(jnp.float32)
    return own + a + b


def whole(far_left, far_right):
    return jnp.concatenate([far_left, far_right], axis=1)


def plane_gather(rows):
    a, b, left, right = ring_gather(rows, PLANE_RINGS[0])
    quarter = jnp.concatenate([rows, a, b, whole(left, right)], axis=0)
    a, b, left, right = ring_gather(quarter, PLANE_RINGS[1])
    return jnp.concatenate([quarter, a, b, whole(left, right)], axis=0)


def four(value):
    n = value.shape[0] // 4
    return [value[i * n : (i + 1) * n] for i in range(4)]


def plane_reduce(rows):
    half = rows.shape[1] // 2
    for back in (PLANE_BACK[1], PLANE_BACK[0]):
        own, a, b, far = four(rows)
        rows = ring_reduce(own, a, b, far[:, :half], far[:, half:], back)
    return rows


def expert_rows(rows, w_gate, w_up, w_down):
    gate = jnp.dot(rows, w_gate, preferred_element_type=jnp.float32)
    upper = jnp.dot(rows, w_up, preferred_element_type=jnp.float32)
    acts = (jax.nn.silu(gate) * upper).astype(jnp.bfloat16)
    return jnp.dot(acts, w_down, preferred_element_type=jnp.float32)


def per_device(
    hidden, expert_ids, gate_logits, accept_len, w_gate, w_up, w_down, draft_in, draft_out
):
    f32, bf16 = jnp.float32, jnp.bfloat16
    local_rows, width = hidden.shape
    half = width // 2
    g, e = lax.axis_index("group"), lax.axis_index("expert")
    z, core = e // 2, e % 2
    columns = EXPERTS * CAP

    keep = jnp.arange(local_rows, dtype=jnp.int32) % DRAFT >= jnp.repeat(accept_len, DRAFT)
    student_in = jnp.where(keep[:, None], hidden, jnp.zeros_like(hidden))

    relative = expert_ids ^ (g * 4 + z // 2)
    pairs = relative.reshape(-1)
    onehot = (pairs[:, None] == jnp.arange(EXPERTS, dtype=jnp.int32)[None, :]).astype(jnp.int32)
    before = jnp.cumsum(onehot, axis=0) - onehot
    slot_index = jnp.sum(before * onehot, axis=1)
    target_column = pairs * CAP + slot_index
    chosen = (target_column[:, None] == jnp.arange(columns, dtype=jnp.int32)[None, :]).astype(f32)
    chosen = chosen.reshape(local_rows, 2, columns)
    dispatch_table = jnp.sum(chosen, axis=1).T.astype(bf16)
    outgoing = jnp.dot(dispatch_table, hidden, preferred_element_type=f32).astype(bf16)
    outgoing = outgoing.reshape(EXPERTS, CAP, width)

    def exchange(k):
        return lambda g, z, c, x, h: (g ^ (k >> 2), z ^ (2 * (k & 3)), c, x, h)

    arrived = [outgoing[0]] + [permute(outgoing[k], exchange(k)) for k in range(1, EXPERTS)]
    own = jnp.concatenate(arrived, axis=0)

    inputs = plane_gather(student_in)

    a1, b1, left, right = ring_gather(own, BLOCK_RINGS[0])
    quarter = jnp.concatenate([own, a1, b1, whole(left, right)], axis=0)
    quarter_x = permute(quarter, other_core)
    a2, b2, left, right = ring_gather(quarter, BLOCK_RINGS[1])
    far = whole(left, right)
    a2_x, b2_x, far_x = [permute(v, other_core) for v in (a2, b2, far)]

    n = quarter.shape[0]
    weights = (w_gate, w_up, w_down)
    t1 = expert_rows(jnp.concatenate([quarter, quarter_x], axis=0), *weights)
    t2 = expert_rows(jnp.concatenate([a2, b2, a2_x, b2_x], axis=0), *weights)
    t3 = expert_rows(jnp.concatenate([far, far_x], axis=0), *weights)

    def with_core(mine, theirs):
        return mine + permute(theirs.astype(bf16), other_core).astype(f32)

    s_far = with_core(t3[:n], t3[n:])
    s_a = with_core(t2[:n], t2[2 * n : 3 * n])
    s_b = with_core(t2[n : 2 * n], t2[3 * n :])
    s_quarter = with_core(t1[:n], t1[n:])
    s_quarter = ring_reduce(s_quarter, s_a, s_b, s_far[:, :half], s_far[:, half:], BLOCK_BACK[1])
    own_s, a_s, b_s, far_s = four(s_quarter)
    summed = ring_reduce(own_s, a_s, b_s, far_s[:, :half], far_s[:, half:], BLOCK_BACK[0])
    summed = summed.astype(bf16).reshape(EXPERTS, CAP, width)
    returned = [summed[0]] + [permute(summed[k], exchange(k)) for k in range(1, EXPERTS)]
    expert_out = jnp.concatenate(returned, axis=0).astype(f32)

    inner = jnp.dot(inputs, draft_in, preferred_element_type=f32)
    active_rows = jax.nn.silu(inner).astype(bf16)
    guess = plane_reduce(jnp.dot(active_rows, draft_out, preferred_element_type=f32))

    rejected = jnp.full((8, 128), jnp.sum(DRAFT - accept_len).astype(f32))
    for move in (
        other_core, x_step(2), y_step(2), z_step(4), z_swap,
        lambda g, z, c, x, h: (g, z ^ 2, c, x, h),
        lambda g, z, c, x, h: (g, z, c, x ^ 1, h),
        lambda g, z, c, x, h: (1 - g, z, c, x, h),
    ):
        rejected = rejected + permute(rejected, move)
    rejected = rejected[:1, :1]

    first_gate = 1.0 / (1.0 + jnp.exp(gate_logits[:, 1] - gate_logits[:, 0]))
    second_gate = 1.0 / (1.0 + jnp.exp(gate_logits[:, 0] - gate_logits[:, 1]))
    gate_pair = jnp.stack([first_gate, second_gate], axis=1)
    combine_table = jnp.sum(chosen * gate_pair[:, :, None], axis=1)
    combined = jnp.dot(
        combine_table, expert_out, precision=lax.Precision.HIGHEST, preferred_element_type=f32
    )
    verified = (hidden.astype(f32) + combined).astype(bf16)
    target = combined.astype(bf16).astype(f32)
    teacher = jnp.where(keep[:, None], target, jnp.zeros_like(target))

    slope = plane_gather((guess - teacher).astype(bf16))
    grad_out = lax.dot_general(
        active_rows, slope, (((0,), (0,)), ((), ())), preferred_element_type=f32
    )
    back_inner = lax.dot_general(
        slope, draft_out, (((1,), (1,)), ((), ())), preferred_element_type=f32
    )
    sigma = jax.nn.sigmoid(inner)
    delta = (back_inner * sigma * (1.0 + inner * (1.0 - sigma))).astype(bf16)
    grad_in = lax.dot_general(delta, inputs, (((0,), (0,)), ((), ())), preferred_element_type=f32)

    mine = jnp.where(core == 0, grad_in, grad_out)
    theirs = jnp.where(core == 0, grad_out, grad_in)
    grad = (mine + permute(theirs.astype(bf16), other_core).astype(f32)).astype(bf16)
    part = width // 8

    def piece(value, at):
        return lax.dynamic_slice_in_dim(value, (at % 8) * part, part, 1)

    total = piece(grad, z).astype(f32)
    for k in range(1, 8):
        total = total + permute(piece(grad, z + k), z_step(k)).astype(f32)
    old = piece(jnp.where(core == 0, draft_in.T, draft_out), z).astype(f32)
    new = (old - (LEARNING_RATE * 2.0 / rejected) * total).astype(bf16)
    gathered = jnp.zeros((new.shape[0], width), bf16)
    gathered = lax.dynamic_update_slice_in_dim(gathered, new, z * part, 1)
    for k in range(1, 8):
        gathered = lax.dynamic_update_slice_in_dim(
            gathered, permute(new, z_step(k)), ((z - k) % 8) * part, 1
        )
    other = permute(gathered, other_core)
    new_in = jnp.where(core == 0, gathered, other).T
    new_out = jnp.where(core == 0, other, gathered)
    return (verified, new_in, new_out)


def solution(mesh):
    return jax.shard_map(
        per_device,
        mesh=mesh,
        in_specs=(
            P(AXES, None),
            P(AXES, None),
            P(AXES, None),
            P(AXES),
            P(None, AXES),
            P(None, AXES),
            P(AXES, None),
            P(None, ("group", "shard")),
            P(("group", "shard"), None),
        ),
        out_specs=(
            P(AXES, None),
            P(None, ("group", "shard")),
            P(("group", "shard"), None),
        ),
        check_vma=False,
    )
```

```python
import itertools

import jax
import jax.numpy as jnp
from jax import lax
from jax.experimental import pallas as pl
from jax.experimental.pallas import tpu as pltpu
from jax.sharding import PartitionSpec as P

EXPERTS = 8
DRAFT = 5
CAP = 3
LEARNING_RATE = 0.5
AXES = ("group", "expert", "shard")
PARTS = (2, 8, 2, 4, 2)


def flat(place):
    index = 0
    for size, at in zip(PARTS, place):
        index = index * size + at
    return index


def permute(value, move):
    pairs = []
    for place in itertools.product(*(range(size) for size in PARTS)):
        pairs.append((flat(place), flat(move(*place))))
    return lax.ppermute(value, AXES, pairs)


def other_core(g, z, c, x, h):
    return g, z, 1 - c, x, h


def x_step(by):
    return lambda g, z, c, x, h: (g, z, c, (x + by) % 4, h)


def y_step(by):
    def move(g, z, c, x, h):
        y = (2 * h + g + by) % 4
        return y % 2, z, c, x, y // 2

    return move


def z_step(by):
    return lambda g, z, c, x, h: (g, (z + by) % 8, c, x, h)


def z_swap(g, z, c, x, h):
    return g, z ^ 1, c, x, h


def h_swap(g, z, c, x, h):
    return g, z, c, x, 1 - h


def by_core(first, second):
    return lambda g, z, c, x, h: (second if c else first)(g, z, c, x, h)


X_RING = (x_step(1), x_step(-1), x_step(1), x_step(-1), x_step(2))
X_BACK = (x_step(-1), x_step(1), x_step(-1), x_step(1), x_step(2))
Y_RING = (y_step(1), y_step(-1), y_step(1), y_step(-1), y_step(2))
Y_BACK = (y_step(-1), y_step(1), y_step(-1), y_step(1), y_step(2))
SQUARE = (z_swap, h_swap, h_swap, z_swap, lambda g, z, c, x, h: (g, z ^ 1, c, x, 1 - h))


def mixed(first, second):
    return tuple(by_core(a, b) for a, b in zip(first, second))


BLOCK_RINGS = (mixed(SQUARE, X_RING), mixed(X_RING, SQUARE))
BLOCK_BACK = (mixed(SQUARE, X_BACK), mixed(X_BACK, SQUARE))
PLANE_RINGS = (mixed(X_RING, Y_RING), mixed(Y_RING, X_RING))
PLANE_BACK = (mixed(X_BACK, Y_BACK), mixed(Y_BACK, X_BACK))
VMEM_LIMIT = 60 * 1024 * 1024
PACK = 3


def kernel_call(body, outs, *args, scalars=(), scratch=()):
    specs = [pl.BlockSpec(memory_space=pltpu.SMEM)] * len(scalars)
    specs += [pl.BlockSpec(memory_space=pltpu.VMEM)] * len(args)
    many = isinstance(outs, (list, tuple))
    spec = pl.BlockSpec(memory_space=pltpu.VMEM)
    return pl.pallas_call(
        body,
        out_shape=outs,
        in_specs=specs,
        out_specs=[spec] * len(outs) if many else spec,
        scratch_shapes=list(scratch),
        compiler_params=pltpu.CompilerParams(vmem_limit_bytes=VMEM_LIMIT),
    )(*scalars, *args)


def like(*shape, dtype=jnp.bfloat16):
    return jax.ShapeDtypeStruct(shape, dtype)


def dot(a, b, contract, precision=None):
    return lax.dot_general(
        a, b, (contract, ((), ())), precision=precision, preferred_element_type=jnp.float32
    )


NN, NT, TN = ((1,), (0,)), ((1,), (1,)), ((0,), (0,))


def far_parts(value):
    half = value.shape[1] // 2
    return value[:, :half], value[:, half:]


def ring_near(value, ring):
    return [permute(value, ring[i]) for i in (0, 1, 4)]


def ring_wide(value, ring):
    half = value.shape[1] // 2
    a, b = permute(value, ring[0]), permute(value, ring[1])
    return a, b, permute(a[:, :half], ring[2]), permute(b[:, half:], ring[3])


def total_of(*parts):
    return sum(p.astype(jnp.float32) for p in parts).astype(jnp.bfloat16)


def ring_near_sum(own, a, b, far, back):
    return total_of(own, permute(a, back[0]), permute(b, back[1]), permute(far, back[4]))


def ring_wide_sum(own, a, b, far_left, far_right, back):
    left, right = permute(far_left, back[2]), permute(far_right, back[3])
    half = left.shape[1]
    a = jnp.concatenate([total_of(a[:, :half], left), a[:, half:]], axis=1)
    b = jnp.concatenate([b[:, :half], total_of(b[:, half:], right)], axis=1)
    return total_of(own, permute(a, back[0]), permute(b, back[1]))


def place(shape, pieces):
    def body(*refs):
        for ref, (_, row, column) in zip(refs[:-1], pieces):
            n, m = ref.shape
            refs[-1][row : row + n, column : column + m] = ref[...]

    return kernel_call(body, like(*shape), *[p for p, _, _ in pieces])


def joined(*rows):
    n, m = rows[0].shape
    return place((n * len(rows), m), [(r, i * n, 0) for i, r in enumerate(rows)])


def rows_of(pieces):
    def body(*refs):
        wide = refs[-1]
        for k, ref in enumerate(refs[:-2]):
            wide[k * CAP : (k + 1) * CAP] = ref[...].astype(jnp.float32)
        refs[-2][...] = wide[...].astype(jnp.bfloat16)

    n, width = len(pieces) * CAP, pieces[0].shape[1]
    return kernel_call(
        body, like(n, width), *pieces, scratch=[pltpu.VMEM((n, width), jnp.float32)]
    )


def slots(ids, lanes):
    f32 = jnp.float32
    slot = lax.broadcasted_iota(jnp.int32, (EXPERTS * CAP, lanes), 0)
    expert, place_in = slot // CAP, slot % CAP
    named = (ids[0:1] == expert) | (ids[1:2] == expert)
    at = lax.broadcasted_iota(jnp.int32, (lanes, lanes), 0)
    to = lax.broadcasted_iota(jnp.int32, (lanes, lanes), 1)
    earlier = jnp.where((at < to) & (at // 10 == to // 10), 1.0, 0.0).astype(jnp.bfloat16)
    before = dot(jnp.where(named, 1.0, 0.0).astype(jnp.bfloat16), earlier, NN)
    return jnp.where(named & (before == place_in.astype(f32)), 1.0, 0.0), expert


def send_body(ids_ref, keep_ref, hidden_ref, out_ref, packed_ref):
    rows, width = hidden_ref.shape
    part = width // PACK
    taken, _ = slots(ids_ref[...], 32)
    table = taken[:, :rows].astype(jnp.bfloat16)
    out_ref[...] = dot(table, hidden_ref[...], NN).astype(jnp.bfloat16)
    to = lax.broadcasted_iota(jnp.int32, (32, rows), 0)
    row = lax.broadcasted_iota(jnp.int32, (32, rows), 1)
    keep = keep_ref[:, :rows]
    count = jnp.sum(keep)
    total = jnp.where(lax.broadcasted_iota(jnp.int32, (32, part), 0) == 30, count, 0.0)
    for j in range(PACK):
        pick = jnp.where(to == row + 10 * j, keep, 0.0).astype(jnp.bfloat16)
        total += dot(pick, hidden_ref[:, j * part : (j + 1) * part], NN)
    packed_ref[...] = total.astype(jnp.bfloat16)


def combine_body(*refs):
    ids_ref, logit_ref, keep_ref, hidden_ref, guess_ref = refs[:5]
    pieces, (verified_ref, slope_ref, wide) = refs[5:13], refs[13:]
    rows, width = hidden_ref.shape
    part = width // PACK
    f32 = jnp.float32
    for k, ref in enumerate(pieces):
        wide[k * CAP : (k + 1) * CAP] = ref[...].astype(f32)
    ids = ids_ref[...]
    taken, expert = slots(ids, 32)
    zero, one = logit_ref[0:1], logit_ref[1:2]
    first, second = 1.0 / (1.0 + jnp.exp(one - zero)), 1.0 / (1.0 + jnp.exp(zero - one))
    gated = taken * jnp.where(ids[0:1] == expert, first, second)
    combined = dot(gated[:, :rows], wide[...], TN, lax.Precision.HIGHEST)
    verified_ref[...] = (hidden_ref[...].astype(f32) + combined).astype(jnp.bfloat16)
    lane = lax.broadcasted_iota(jnp.int32, gated.shape, 1)
    kept = gated * keep_ref[...]
    teacher = jnp.zeros((32, part), f32)
    for j in range(PACK):
        table = jnp.where((lane >= 10 * j) & (lane < 10 * j + 10), kept, 0.0)
        teacher += dot(table, wide[:, j * part : (j + 1) * part], TN, lax.Precision.HIGHEST)
    teacher = teacher.astype(jnp.bfloat16).astype(f32)
    slope_ref[...] = (guess_ref[...].astype(f32) - teacher).astype(jnp.bfloat16)


def expert_body(*refs):
    n = (len(refs) - 4) // 2
    pieces, (gate_ref, up_ref, down_ref), outs, rows = (
        refs[:n], refs[n : n + 3], refs[n + 3 : 2 * n + 3], refs[-1],
    )
    at = 0
    for ref in pieces:
        if len(ref.shape) == 3:
            half = ref.shape[2]
            rows[at : at + ref.shape[1], :half] = ref[0]
            rows[at : at + ref.shape[1], half:] = ref[1]
        else:
            rows[at : at + ref.shape[0], :] = ref[...]
        at += ref.shape[-2]
    gate = dot(rows[...], gate_ref[...], NN)
    upper = dot(rows[...], up_ref[...], NN)
    acts = (gate / (1.0 + jnp.exp(-gate)) * upper).astype(jnp.bfloat16)
    width = down_ref.shape[1]
    step = width // 6
    for i in range(6):
        out = dot(acts, down_ref[:, i * step : (i + 1) * step], NN).astype(jnp.bfloat16)
        at = 0
        for ref in outs:
            ref[:, i * step : (i + 1) * step] = out[at : at + ref.shape[0]]
            at += ref.shape[0]


def expert_rows(pieces, w_gate, w_up, w_down):
    width = w_gate.shape[0]
    rows = sum(p.shape[0] for p in pieces)
    return kernel_call(
        expert_body,
        [like(p.shape[0], width) for p in pieces],
        *pieces, w_gate, w_up, w_down,
        scratch=[pltpu.VMEM((rows, width), jnp.bfloat16)],
    )


def shifted(value, by):
    return pltpu.roll(value, by % value.shape[0], 0) if by else value


def fill(target, pieces):
    quarter, a, b, left, right = pieces
    n, half = quarter.shape[0], left.shape[1]
    target[:n], target[n : 2 * n], target[2 * n : 3 * n] = quarter[...], a[...], b[...]
    target[3 * n :, :half], target[3 * n :, half:] = left[...], right[...]


def forward_body(*refs):
    pieces, (in_ref, out_ref), (x_ref, inner_ref, guess_ref) = refs[:5], refs[5:7], refs[7:]
    fill(x_ref, pieces)
    rows, part = x_ref.shape
    x = x_ref[...]
    inner = jnp.zeros(inner_ref.shape, jnp.float32)
    for j in range(PACK):
        inner += shifted(dot(x, in_ref[:, j * part : (j + 1) * part], NT), -10 * j)
    row = lax.broadcasted_iota(jnp.int32, inner.shape, 0) % 32
    inner = jnp.where(row < 10, inner, 0.0)
    inner_ref[...] = inner
    active = inner / (1.0 + jnp.exp(-inner))
    guess = jnp.zeros((rows, part), jnp.float32)
    for j in range(PACK):
        act = shifted(active, 10 * j).astype(jnp.bfloat16)
        guess += dot(act, out_ref[:, j * part : (j + 1) * part], NN)
    guess_ref[...] = guess.astype(jnp.bfloat16)


def backward_body(*refs):
    core_ref, pieces, (x_ref, inner_ref, out_ref), (mine_ref, theirs_ref, slope) = (
        refs[0], refs[1:6], refs[6:9], refs[9:],
    )
    fill(slope, pieces)
    rows, part = x_ref.shape
    units = inner_ref.shape[1]
    piece = part // 8
    inner = inner_ref[...]
    sigma = 1.0 / (1.0 + jnp.exp(-inner))
    active = inner * sigma
    back = jnp.zeros(inner.shape, jnp.float32)
    for j in range(PACK):
        back += shifted(dot(slope[...], out_ref[:, j * part : (j + 1) * part], NT), -10 * j)
    row = lax.broadcasted_iota(jnp.int32, inner.shape, 0) % 32
    delta = jnp.where(row < 10, back * sigma * (1.0 + inner * (1.0 - sigma)), 0.0)
    core = core_ref[0]
    lane = lax.broadcasted_iota(jnp.int32, (rows, piece), 0) % 32
    count = jnp.sum(
        jnp.where(lane == 30, x_ref[:, :piece].astype(jnp.float32), 0.0), axis=0, keepdims=True
    )
    high = jnp.floor(count * 0.0625)
    line = lax.broadcasted_iota(jnp.int32, (8, piece), 0)
    tail = jnp.where(line == 0, high, jnp.where(line == 1, count - 16.0 * high, 0.0))
    tail = tail.astype(jnp.bfloat16)

    def put(ref, left, right):
        for j in range(PACK):
            grad = dot(shifted(left, 10 * j).astype(jnp.bfloat16), right[...], TN)
            grad = grad.astype(jnp.bfloat16)
            for i in range(8):
                ref[i, j * units : (j + 1) * units, :] = grad[:, i * piece : (i + 1) * piece]
        for i in range(8):
            ref[i, PACK * units :, :] = tail

    @pl.when(core == 0)
    def _():
        put(mine_ref, delta, x_ref)
        put(theirs_ref, active, slope)

    @pl.when(core == 1)
    def _():
        put(theirs_ref, delta, x_ref)
        put(mine_ref, active, slope)


def turn_body(z_ref, mine_ref, other_ref, *outs):
    for k, out in enumerate(outs):
        at = (z_ref[0] + k) % 8
        total = mine_ref[at].astype(jnp.float32) + other_ref[at].astype(jnp.float32)
        out[...] = total.astype(jnp.bfloat16)


def update_body(core_ref, z_ref, *refs):
    pieces, (in_ref, out_ref), new_ref = refs[:8], refs[8:10], refs[10]
    total = pieces[0][...].astype(jnp.float32)
    for ref in pieces[1:]:
        total += ref[...].astype(jnp.float32)
    rows, piece = new_ref.shape
    units, part = rows // PACK, in_ref.shape[1] // PACK
    rejected = 16.0 * total[rows : rows + 1] + total[rows + 1 : rows + 2]
    rate = (2.0 * LEARNING_RATE) / rejected
    in_core = jnp.full((units, piece), core_ref[0], jnp.int32) == 0
    for j in range(PACK):
        columns = pl.ds(pl.multiple_of(j * part + z_ref[0] * piece, piece), piece)
        old = jnp.where(
            in_core, in_ref[:, columns].astype(jnp.float32), out_ref[:, columns].astype(jnp.float32)
        )
        new = old - rate * total[j * units : (j + 1) * units]
        new_ref[j * units : (j + 1) * units] = new.astype(jnp.bfloat16)


def spread_body(z_ref, *refs):
    pieces, out_ref = refs[:8], refs[8]
    rows, piece = pieces[0].shape
    units, part = rows // PACK, out_ref.shape[1] // PACK
    for k, ref in enumerate(pieces):
        at = (z_ref[0] + 8 - k) % 8
        for j in range(PACK):
            columns = pl.ds(pl.multiple_of(j * part + at * piece, piece), piece)
            out_ref[:, columns] = ref[j * units : (j + 1) * units]


def per_device(
    hidden, expert_ids, gate_logits, accept_len, w_gate, w_up, w_down, draft_in, draft_out
):
    local_rows, width = hidden.shape
    part, units = width // PACK, draft_out.shape[0]
    g, e = lax.axis_index("group"), lax.axis_index("expert")
    z, core = (e // 2).astype(jnp.int32).reshape(1), (e % 2).astype(jnp.int32).reshape(1)

    def lanes(rows, empty):
        return jnp.pad(jnp.tile(rows, (1, PACK)), ((0, 0), (0, 2)), constant_values=empty)

    keep = jnp.arange(local_rows, dtype=jnp.int32) % DRAFT >= jnp.repeat(accept_len, DRAFT)
    keep = lanes(keep.astype(jnp.float32)[None], 0.0)
    ids = lanes((expert_ids ^ (g * 4 + e // 4)).T, EXPERTS)
    logits = lanes(gate_logits.T, 0.0)

    outgoing, packed = kernel_call(
        send_body, [like(EXPERTS * CAP, width), like(32, part)], ids, keep, hidden
    )
    outgoing = outgoing.reshape(EXPERTS, CAP, width)

    def exchange(k):
        return lambda g, z, c, x, h: (g ^ (k >> 2), z ^ (2 * (k & 3)), c, x, h)

    own = rows_of(
        [outgoing[0]] + [permute(outgoing[k], exchange(k)) for k in range(1, EXPERTS)]
    )

    quarter = joined(packed, *ring_near(packed, PLANE_RINGS[0]))
    x, inner, guess = kernel_call(
        forward_body,
        [like(512, part), like(512, units, dtype=jnp.float32), like(512, part)],
        quarter, *ring_wide(quarter, PLANE_RINGS[1]), draft_in.T, draft_out,
    )

    weights = (w_gate, w_up, w_down)
    block = joined(own, *ring_near(own, BLOCK_RINGS[0]))
    a, b, left, right = ring_wide(block, BLOCK_RINGS[1])
    far = place(block.shape, [(left, 0, 0), (right, 0, width // 2)])
    block_t, block_o = expert_rows([block, permute(block, other_core)], *weights)
    a_t, b_t, a_o, b_o = expert_rows(
        [a, b, permute(a, other_core), permute(b, other_core)], *weights
    )
    far_t, far_o = expert_rows([far, permute(far, other_core)], *weights)

    far_s = total_of(far_t, permute(far_o, other_core))
    a_s = total_of(a_t, permute(a_o, other_core))
    b_s = total_of(b_t, permute(b_o, other_core))
    block_s = total_of(block_t, permute(block_o, other_core))
    block_s = ring_wide_sum(block_s, a_s, b_s, *far_parts(far_s), BLOCK_BACK[1])
    n = block_s.shape[0] // 4
    summed = ring_near_sum(*[block_s[i * n : (i + 1) * n] for i in range(4)], BLOCK_BACK[0])
    summed = summed.reshape(EXPERTS, CAP, width)
    returned = [summed[0]] + [permute(summed[k], exchange(k)) for k in range(1, EXPERTS)]

    n = 128
    guess = ring_wide_sum(
        guess[:n], guess[n : 2 * n], guess[2 * n : 3 * n], *far_parts(guess[3 * n :]),
        PLANE_BACK[1],
    )
    guess = ring_near_sum(*[guess[i * 32 : (i + 1) * 32] for i in range(4)], PLANE_BACK[0])

    verified, slope = kernel_call(
        combine_body,
        [like(local_rows, width), like(32, part)],
        ids, logits, keep, hidden, guess, *returned,
        scratch=[pltpu.VMEM((EXPERTS * CAP, width), jnp.float32)],
    )

    slope = joined(slope, *ring_near(slope, PLANE_RINGS[0]))
    shape = (8, PACK * units + 8, part // 8)
    mine, theirs = kernel_call(
        backward_body,
        [like(*shape), like(*shape)],
        slope, *ring_wide(slope, PLANE_RINGS[1]), x, inner, draft_out,
        scalars=(core,),
        scratch=[pltpu.VMEM((512, part), jnp.bfloat16)],
    )

    turned = kernel_call(
        turn_body, [like(*shape[1:])] * 8, mine, permute(theirs, other_core), scalars=(z,)
    )
    pieces = [turned[0]] + [permute(turned[k], z_step(k)) for k in range(1, 8)]
    new = kernel_call(
        update_body, like(PACK * units, shape[2]), *pieces, draft_in.T, draft_out,
        scalars=(core, z),
    )
    pieces = [new] + [permute(new, z_step(k)) for k in range(1, 8)]
    gathered = kernel_call(spread_body, like(units, width), *pieces, scalars=(z,))
    other = permute(gathered, other_core)
    in_core = core[0] == 0
    new_in = jnp.where(in_core, gathered, other).T
    new_out = jnp.where(in_core, other, gathered)
    return (verified, new_in, new_out)


def solution(mesh):
    return jax.shard_map(
        per_device,
        mesh=mesh,
        in_specs=(
            P(AXES, None),
            P(AXES, None),
            P(AXES, None),
            P(AXES),
            P(None, AXES),
            P(None, AXES),
            P(AXES, None),
            P(None, ("group", "shard")),
            P(("group", "shard"), None),
        ),
        out_specs=(
            P(AXES, None),
            P(None, ("group", "shard")),
            P(("group", "shard"), None),
        ),
        check_vma=False,
    )
```

```python
import itertools
import math

import jax
import jax.numpy as jnp
from jax import lax
from jax.experimental import pallas as pl
from jax.experimental.pallas import tpu as pltpu
from jax.sharding import PartitionSpec as P

EXPERTS = 8
DRAFT = 5
CAP = 3
LEARNING_RATE = 0.5
AXES = ("y_lo", "z_pair", "z_in", "core", "x", "y_hi")
SIZES = (2, 4, 2, 2, 4, 2)
OWNERS = ("y_lo", "z_pair")
PLANE = ("y_lo", "x", "y_hi")
PARTS = (2, 8, 2, 4, 2)


def flat(place):
    index = 0
    for size, at in zip(PARTS, place):
        index = index * size + at
    return index


def permute(value, move):
    pairs = []
    for place in itertools.product(*(range(size) for size in PARTS)):
        pairs.append((flat(place), flat(move(*place))))
    return lax.ppermute(value, AXES, pairs)


def other_core(g, z, c, x, h):
    return g, z, 1 - c, x, h


def x_step(by):
    return lambda g, z, c, x, h: (g, z, c, (x + by) % 4, h)


def y_step(by):
    def move(g, z, c, x, h):
        y = (2 * h + g + by) % 4
        return y % 2, z, c, x, y // 2

    return move


def z_step(by):
    return lambda g, z, c, x, h: (g, (z + by) % 8, c, x, h)


def z_swap(g, z, c, x, h):
    return g, z ^ 1, c, x, h


def h_swap(g, z, c, x, h):
    return g, z, c, x, 1 - h


def by_core(first, second):
    return lambda g, z, c, x, h: (second if c else first)(g, z, c, x, h)


X_RING = (x_step(1), x_step(-1), x_step(1), x_step(-1), x_step(2))
X_BACK = (x_step(-1), x_step(1), x_step(-1), x_step(1), x_step(2))
Y_RING = (y_step(1), y_step(-1), y_step(1), y_step(-1), y_step(2))
Y_BACK = (y_step(-1), y_step(1), y_step(-1), y_step(1), y_step(2))
SQUARE = (z_swap, h_swap, h_swap, z_swap, lambda g, z, c, x, h: (g, z ^ 1, c, x, 1 - h))


def mixed(first, second):
    return tuple(by_core(a, b) for a, b in zip(first, second))


BLOCK_RINGS = (mixed(SQUARE, X_RING), mixed(X_RING, SQUARE))
BLOCK_BACK = (mixed(SQUARE, X_BACK), mixed(X_BACK, SQUARE))
PLANE_RINGS = (mixed(X_RING, Y_RING), mixed(Y_RING, X_RING))
PLANE_BACK = (mixed(X_BACK, Y_BACK), mixed(Y_BACK, X_BACK))
LARGE, SMALL = 32 * 1024 * 1024, 12 * 1024 * 1024
IN_VMEM = True
PACK = 3


def kernel_call(body, outs, *args, scalars=(), scratch=(), after=(), limit=SMALL, flops=0):
    many = isinstance(outs, (list, tuple))
    listed = list(outs) if many else [outs]
    first, last = len(scalars), len(scalars) + len(args)

    def run(*refs):
        body(*refs[:last], *refs[last + len(after) :])

    if IN_VMEM:
        args = [pltpu.with_memory_space_constraint(a, pltpu.VMEM) for a in args]
    size = sum(math.prod(a.shape) * jnp.dtype(a.dtype).itemsize for a in (*args, *listed))
    out = pl.pallas_call(
        run,
        out_shape=listed if many else outs,
        in_specs=[pl.BlockSpec(memory_space=pltpu.SMEM)] * first
        + [pl.BlockSpec(memory_space=pltpu.VMEM)] * (last - first)
        + [pl.BlockSpec(memory_space=pl.ANY)] * len(after),
        out_specs=[pl.BlockSpec(memory_space=pltpu.VMEM)] * len(listed)
        if many
        else pl.BlockSpec(memory_space=pltpu.VMEM),
        scratch_shapes=list(scratch),
        compiler_params=pltpu.CompilerParams(vmem_limit_bytes=limit),
        cost_estimate=pl.CostEstimate(flops=flops, bytes_accessed=size, transcendentals=0),
    )(*scalars, *args, *after)
    return out


def like(*shape, dtype=jnp.bfloat16):
    if IN_VMEM:
        return pltpu.VMEM(shape, dtype)
    return jax.ShapeDtypeStruct(shape, dtype)


def in_hbm(*shape, dtype=jnp.bfloat16):
    return jax.ShapeDtypeStruct(shape, dtype)


def dot(a, b, contract, precision=None):
    return lax.dot_general(
        a, b, (contract, ((), ())), precision=precision, preferred_element_type=jnp.float32
    )


NN, NT, TN = ((1,), (0,)), ((1,), (1,)), ((0,), (0,))


def f32(value):
    return value.astype(jnp.float32)


def near(value, ring):
    return [permute(value, ring[i]) for i in (0, 1, 4)]


def joined(pieces, after=()):
    n, m = pieces[0].shape

    def body(*refs):
        for i, ref in enumerate(refs[:-1]):
            refs[-1][i * n : (i + 1) * n] = ref[...]

    return kernel_call(body, like(n * len(pieces), m), *pieces, after=after)


def halves(a, b, after=()):
    n, m = a.shape
    half = m // 2

    def body(a_ref, b_ref, left, right):
        left[...], right[...] = a_ref[:, :half], b_ref[:, half:]

    return kernel_call(body, [like(n, half)] * 2, a, b, after=after)


def halves_of_sum(a, b):
    n, m = a.shape
    half = m // 2

    def body(a_ref, b_ref, left, right):
        total = (f32(a_ref[...]) + f32(b_ref[...])).astype(jnp.bfloat16)
        left[...], right[...] = total[:, :half], total[:, half:]

    return kernel_call(body, [like(n, half)] * 2, a, b)


def passed_on(a, b, left, right, after=()):
    n, m = a[0].shape
    half, count = m // 2, len(a)

    def body(*refs):
        ins, outs = refs[: 2 * count + 2], refs[2 * count + 2 :]
        for parts, far, out, where in (
            (ins[:count], ins[-2], outs[0], slice(0, half)),
            (ins[count : 2 * count], ins[-1], outs[1], slice(half, m)),
        ):
            other = slice(half, m) if where.start == 0 else slice(0, half)
            out[:, where] = (sum(f32(p[:, where]) for p in parts) + f32(far[...])).astype(
                jnp.bfloat16
            )
            out[:, other] = sum(f32(p[:, other]) for p in parts).astype(jnp.bfloat16)

    return kernel_call(body, [like(n, m)] * 2, *a, *b, left, right, after=after)


def quarters_of_sum(parts, after=()):
    n, m = parts[0].shape
    n //= 4

    def body(*refs):
        for i, out in enumerate(refs[-4:]):
            rows = slice(i * n, (i + 1) * n)
            out[...] = sum(f32(p[rows]) for p in refs[:-4]).astype(jnp.bfloat16)

    return kernel_call(body, [like(n, m)] * 4, *parts, after=after)


def rows_of(pieces):
    count, width = pieces.shape[0] * CAP, pieces.shape[2]

    def body(in_ref, out_ref, wide):
        for k in range(EXPERTS):
            wide[k * CAP : (k + 1) * CAP] = f32(in_ref[k])
        out_ref[...] = wide[...].astype(jnp.bfloat16)

    return kernel_call(
        body, like(count, width), pieces, scratch=[pltpu.VMEM((count, width), jnp.float32)]
    )


def pieces_of_sum(parts):
    count, width = parts[0].shape

    def body(*refs):
        ins, (out_ref, wide) = refs[:-2], refs[-2:]
        wide[...] = sum(f32(p[...]) for p in ins)
        for k in range(EXPERTS):
            out_ref[k] = wide[k * CAP : (k + 1) * CAP].astype(jnp.bfloat16)

    return kernel_call(
        body, like(EXPERTS, CAP, width), *parts,
        scratch=[pltpu.VMEM((count, width), jnp.float32)],
    )


def slots(ids, lanes):
    slot = lax.broadcasted_iota(jnp.int32, (EXPERTS * CAP, lanes), 0)
    expert, place_in = slot // CAP, slot % CAP
    named = (ids[0:1] == expert) | (ids[1:2] == expert)
    at = lax.broadcasted_iota(jnp.int32, (lanes, lanes), 0)
    to = lax.broadcasted_iota(jnp.int32, (lanes, lanes), 1)
    earlier = jnp.where((at < to) & (at // 10 == to // 10), 1.0, 0.0).astype(jnp.bfloat16)
    before = dot(jnp.where(named, 1.0, 0.0).astype(jnp.bfloat16), earlier, NN)
    return jnp.where(named & (before == f32(place_in)), 1.0, 0.0), expert


def send_body(ids_ref, keep_ref, hidden_ref, out_ref, packed_ref, wide):
    rows, width = hidden_ref.shape
    part = width // PACK
    taken, _ = slots(ids_ref[...], 32)
    table = taken[:, :rows].astype(jnp.bfloat16)
    wide[...] = dot(table, hidden_ref[...], NN)
    for k in range(EXPERTS):
        out_ref[k] = wide[k * CAP : (k + 1) * CAP].astype(jnp.bfloat16)
    to = lax.broadcasted_iota(jnp.int32, (32, rows), 0)
    row = lax.broadcasted_iota(jnp.int32, (32, rows), 1)
    keep = keep_ref[:, :rows]
    count = jnp.sum(keep)
    total = jnp.where(lax.broadcasted_iota(jnp.int32, (32, part), 0) == 30, count, 0.0)
    for j in range(PACK):
        pick = jnp.where(to == row + 10 * j, keep, 0.0).astype(jnp.bfloat16)
        total += dot(pick, hidden_ref[:, j * part : (j + 1) * part], NN)
    packed_ref[...] = total.astype(jnp.bfloat16)


def combine_body(ids_ref, logit_ref, keep_ref, hidden_ref, *refs):
    guess, (returned_ref, verified_ref, slope_ref, wide) = refs[:4], refs[4:]
    rows, width = hidden_ref.shape
    part = width // PACK
    for k in range(EXPERTS):
        wide[k * CAP : (k + 1) * CAP] = f32(returned_ref[k])
    ids = ids_ref[...]
    taken, expert = slots(ids, 32)
    zero, one = logit_ref[0:1], logit_ref[1:2]
    first, second = 1.0 / (1.0 + jnp.exp(one - zero)), 1.0 / (1.0 + jnp.exp(zero - one))
    gated = taken * jnp.where(ids[0:1] == expert, first, second)
    combined = dot(gated[:, :rows], wide[...], TN, lax.Precision.HIGHEST)
    verified_ref[...] = (f32(hidden_ref[...]) + combined).astype(jnp.bfloat16)
    lane = lax.broadcasted_iota(jnp.int32, gated.shape, 1)
    kept = gated * keep_ref[...]
    teacher = jnp.zeros((32, part), jnp.float32)
    for j in range(PACK):
        table = jnp.where((lane >= 10 * j) & (lane < 10 * j + 10), kept, 0.0)
        teacher += dot(table, wide[:, j * part : (j + 1) * part], TN, lax.Precision.HIGHEST)
    teacher = f32(teacher.astype(jnp.bfloat16))
    slope_ref[...] = (sum(f32(g[...]) for g in guess) - teacher).astype(jnp.bfloat16)


def expert_rows(blocks, w_gate, w_up, w_down, after=()):
    width = w_gate.shape[0]
    heights = [block[0].shape[0] for block in blocks]
    flat_blocks = [part for block in blocks for part in block]
    total, count = sum(heights), len(flat_blocks)
    step = width // 6

    def body(*refs):
        ins, (gate_ref, up_ref, down_ref) = list(refs[:count]), refs[count : count + 3]
        outs, rows = refs[count + 3 : -1], refs[-1]
        at = 0
        for block, height in zip(blocks, heights):
            column = 0
            for _ in block:
                ref = ins.pop(0)
                rows[at : at + height, column : column + ref.shape[1]] = ref[...]
                column += ref.shape[1]
            at += height
        gate = dot(rows[...], gate_ref[...], NN)
        upper = dot(rows[...], up_ref[...], NN)
        acts = (gate / (1.0 + jnp.exp(-gate)) * upper).astype(jnp.bfloat16)
        for i in range(6):
            columns = slice(i * step, (i + 1) * step)
            out = dot(acts, down_ref[:, columns], NN).astype(jnp.bfloat16)
            at = 0
            for ref, height in zip(outs, heights):
                ref[:, columns] = out[at : at + height]
                at += height

    return kernel_call(
        body, [like(height, width) for height in heights], *flat_blocks, w_gate, w_up, w_down,
        scratch=[pltpu.VMEM((total, width), jnp.bfloat16)], after=after, limit=LARGE,
        flops=6 * total * width * w_gate.shape[1],
    )


def shifted(value, by):
    return pltpu.roll(value, by % value.shape[0], 0) if by else value


def fill(target, pieces):
    quarter, a, b, left, right = pieces
    n, half = quarter.shape[0], left.shape[1]
    target[:n], target[n : 2 * n], target[2 * n : 3 * n] = quarter[...], a[...], b[...]
    target[3 * n :, :half], target[3 * n :, half:] = left[...], right[...]


def forward_body(*refs):
    pieces, (in_ref, out_ref), (x_ref, inner_ref, *guesses) = refs[:5], refs[5:7], refs[7:]
    fill(x_ref, pieces)
    rows, part = x_ref.shape
    x = x_ref[...]
    inner = jnp.zeros(inner_ref.shape, jnp.float32)
    for j in range(PACK):
        inner += shifted(dot(x, in_ref[:, j * part : (j + 1) * part], NT), -10 * j)
    row = lax.broadcasted_iota(jnp.int32, inner.shape, 0) % 32
    inner = jnp.where(row < 10, inner, 0.0)
    inner_ref[...] = inner
    active = inner / (1.0 + jnp.exp(-inner))
    guess = jnp.zeros((rows, part), jnp.float32)
    for j in range(PACK):
        act = shifted(active, 10 * j).astype(jnp.bfloat16)
        guess += dot(act, out_ref[:, j * part : (j + 1) * part], NN)
    guess = guess.astype(jnp.bfloat16)
    n, half = rows // 4, part // 2
    for i in range(3):
        guesses[i][...] = guess[i * n : (i + 1) * n]
    guesses[3][...], guesses[4][...] = guess[3 * n :, :half], guess[3 * n :, half:]


def backward_body(*refs):
    core_ref, pieces, (x_ref, inner_ref, out_ref), (mine_ref, theirs_ref, slope) = (
        refs[0], refs[1:6], refs[6:9], refs[9:],
    )
    fill(slope, pieces)
    rows, part = x_ref.shape
    units = inner_ref.shape[1]
    piece = part // 8
    inner = inner_ref[...]
    sigma = 1.0 / (1.0 + jnp.exp(-inner))
    active = inner * sigma
    back = jnp.zeros(inner.shape, jnp.float32)
    for j in range(PACK):
        back += shifted(dot(slope[...], out_ref[:, j * part : (j + 1) * part], NT), -10 * j)
    row = lax.broadcasted_iota(jnp.int32, inner.shape, 0) % 32
    delta = jnp.where(row < 10, back * sigma * (1.0 + inner * (1.0 - sigma)), 0.0)
    core = core_ref[0]
    lane = lax.broadcasted_iota(jnp.int32, (rows, piece), 0) % 32
    count = jnp.sum(
        jnp.where(lane == 30, x_ref[:, :piece].astype(jnp.float32), 0.0), axis=0, keepdims=True
    )
    high = jnp.floor(count * 0.0625)
    line = lax.broadcasted_iota(jnp.int32, (8, piece), 0)
    tail = jnp.where(line == 0, high, jnp.where(line == 1, count - 16.0 * high, 0.0))
    tail = tail.astype(jnp.bfloat16)

    def put(ref, left, right):
        for j in range(PACK):
            grad = dot(shifted(left, 10 * j).astype(jnp.bfloat16), right[...], TN)
            grad = grad.astype(jnp.bfloat16)
            for i in range(8):
                ref[i, j * units : (j + 1) * units, :] = grad[:, i * piece : (i + 1) * piece]
        for i in range(8):
            ref[i, PACK * units :, :] = tail

    @pl.when(core == 0)
    def _():
        put(mine_ref, delta, x_ref)
        put(theirs_ref, active, slope)

    @pl.when(core == 1)
    def _():
        put(theirs_ref, delta, x_ref)
        put(mine_ref, active, slope)


def turn_body(z_ref, mine_ref, other_ref, *outs):
    for k, out in enumerate(outs):
        at = (z_ref[0] + k) % 8
        total = mine_ref[at].astype(jnp.float32) + other_ref[at].astype(jnp.float32)
        out[...] = total.astype(jnp.bfloat16)


def update_body(core_ref, z_ref, *refs):
    pieces, (in_ref, out_ref), new_ref = refs[:8], refs[8:10], refs[10]
    total = pieces[0][...].astype(jnp.float32)
    for ref in pieces[1:]:
        total += ref[...].astype(jnp.float32)
    rows, piece = new_ref.shape
    units, part = rows // PACK, in_ref.shape[1] // PACK
    rejected = 16.0 * total[rows : rows + 1] + total[rows + 1 : rows + 2]
    rate = (2.0 * LEARNING_RATE) / rejected
    in_core = jnp.full((units, piece), core_ref[0], jnp.int32) == 0
    for j in range(PACK):
        columns = pl.ds(pl.multiple_of(j * part + z_ref[0] * piece, piece), piece)
        old = jnp.where(
            in_core, in_ref[:, columns].astype(jnp.float32), out_ref[:, columns].astype(jnp.float32)
        )
        new = old - rate * total[j * units : (j + 1) * units]
        new_ref[j * units : (j + 1) * units] = new.astype(jnp.bfloat16)


def spread_body(z_ref, *refs):
    pieces, out_ref = refs[:8], refs[8]
    rows, piece = pieces[0].shape
    units, part = rows // PACK, out_ref.shape[1] // PACK
    for k, ref in enumerate(pieces):
        at = (z_ref[0] + 8 - k) % 8
        for j in range(PACK):
            columns = pl.ds(pl.multiple_of(j * part + at * piece, piece), piece)
            out_ref[:, columns] = ref[j * units : (j + 1) * units]


def per_device(
    hidden, expert_ids, gate_logits, accept_len, w_gate, w_up, w_down, draft_in, draft_out
):
    local_rows, width = hidden.shape
    part, units = width // PACK, draft_out.shape[0]
    core = lax.axis_index("core").astype(jnp.int32).reshape(1)
    z = (2 * lax.axis_index("z_pair") + lax.axis_index("z_in")).astype(jnp.int32).reshape(1)

    def lanes(rows, empty):
        return jnp.pad(jnp.tile(rows, (1, PACK)), ((0, 0), (0, 2)), constant_values=empty)

    keep = jnp.arange(local_rows, dtype=jnp.int32) % DRAFT >= jnp.repeat(accept_len, DRAFT)
    keep = lanes(f32(keep)[None], 0.0)
    ids = lanes(expert_ids.T, EXPERTS)
    logits = lanes(gate_logits.T, 0.0)
    wide = pltpu.VMEM((EXPERTS * CAP, width), jnp.float32)

    outgoing, packed = kernel_call(
        send_body, [like(EXPERTS, CAP, width), like(32, part)], ids, keep, hidden,
        scratch=[wide], flops=4 * 32 * 10 * width,
    )

    def exchange(pieces):
        return lax.all_to_all(pieces, OWNERS, split_axis=0, concat_axis=0, tiled=True)

    inputs = [packed, *near(packed, PLANE_RINGS[0])]
    own = rows_of(exchange(outgoing))
    near_own = near(own, BLOCK_RINGS[0])
    inputs = joined(inputs, after=[own])
    in_a, in_b = [permute(inputs, move) for move in PLANE_RINGS[1][:2]]

    weights = (w_gate, w_up, w_down)
    block = joined([own, *near_own])
    a, b = [permute(block, move) for move in BLOCK_RINGS[1][:2]]
    in_left, in_right = halves(in_a, in_b, after=[block])
    block_t, block_o = expert_rows([[block], [permute(block, other_core)]], *weights)
    in_left, in_right = permute(in_left, PLANE_RINGS[1][2]), permute(in_right, PLANE_RINGS[1][3])

    left, right = halves(a, b, after=[block_t])
    left, right = permute(left, BLOCK_RINGS[1][2]), permute(right, BLOCK_RINGS[1][3])
    a_t, b_t, a_o, b_o = expert_rows(
        [[a], [b], [permute(a, other_core)], [permute(b, other_core)]], *weights
    )
    far_t, far_o = expert_rows(
        [[left, right], [permute(left, other_core), permute(right, other_core)]],
        *weights, after=[a_t],
    )

    left, right = halves_of_sum(far_t, permute(far_o, other_core))
    left, right = permute(left, BLOCK_BACK[1][2]), permute(right, BLOCK_BACK[1][3])
    x, inner, *guess = kernel_call(
        forward_body,
        [like(512, part), like(512, units, dtype=jnp.float32)]
        + [like(128, part)] * 3 + [like(128, part // 2)] * 2,
        inputs, in_a, in_b, in_left, in_right, draft_in.T, draft_out,
        after=[far_t], limit=LARGE, flops=12 * 512 * part * units,
    )
    a, b = passed_on(
        [a_t, permute(a_o, other_core)], [b_t, permute(b_o, other_core)], left, right
    )
    guess_left, guess_right = permute(guess[3], PLANE_BACK[1][2]), permute(guess[4], PLANE_BACK[1][3])
    block = quarters_of_sum(
        [block_t, permute(block_o, other_core), permute(a, BLOCK_BACK[1][0]), permute(b, BLOCK_BACK[1][1])]
    )
    guess_a, guess_b = passed_on(
        guess[1:2], guess[2:3], guess_left, guess_right, after=[block[0]]
    )
    guess_a, guess_b = permute(guess_a, PLANE_BACK[1][0]), permute(guess_b, PLANE_BACK[1][1])
    summed = pieces_of_sum(
        [block[0]] + [permute(block[i], BLOCK_BACK[0][(0, 1, 4)[i - 1]]) for i in (1, 2, 3)]
    )
    guess = quarters_of_sum([guess[0], guess_a, guess_b], after=[summed])
    guess = [guess[0]] + [permute(guess[i], PLANE_BACK[0][(0, 1, 4)[i - 1]]) for i in (1, 2, 3)]

    verified, slope = kernel_call(
        combine_body,
        [in_hbm(local_rows, width), like(32, part)],
        ids, logits, keep, hidden, *guess, exchange(summed), scratch=[wide],
    )

    slope = joined([slope, *near(slope, PLANE_RINGS[0])])
    a, b = [permute(slope, move) for move in PLANE_RINGS[1][:2]]
    left, right = halves(a, b)
    left, right = permute(left, PLANE_RINGS[1][2]), permute(right, PLANE_RINGS[1][3])
    shape = (8, PACK * units + 8, part // 8)
    mine, theirs = kernel_call(
        backward_body,
        [like(*shape), like(*shape)],
        slope, a, b, left, right, x, inner, draft_out,
        scalars=(core,), scratch=[pltpu.VMEM((512, part), jnp.bfloat16)], limit=LARGE,
    )

    turned = kernel_call(
        turn_body, [like(*shape[1:])] * 8, mine, permute(theirs, other_core), scalars=(z,)
    )
    pieces = [turned[0]] + [permute(turned[k], z_step(k)) for k in range(1, 8)]
    new = kernel_call(
        update_body, like(PACK * units, shape[2]), *pieces, draft_in.T, draft_out,
        scalars=(core, z),
    )
    pieces = [new] + [permute(new, z_step(k)) for k in range(1, 8)]
    gathered = kernel_call(spread_body, like(units, width), *pieces, scalars=(z,))
    other = permute(gathered, other_core)
    in_core = core[0] == 0
    new_in = jnp.where(in_core, gathered, other).T
    new_out = jnp.where(in_core, other, gathered)
    return (verified, new_in, new_out)


def solution(mesh):
    return jax.shard_map(
        per_device,
        mesh=jax.sharding.Mesh(mesh.devices.reshape(SIZES), AXES),
        in_specs=(
            P(AXES, None),
            P(AXES, None),
            P(AXES, None),
            P(AXES),
            P(None, AXES),
            P(None, AXES),
            P(AXES, None),
            P(None, PLANE),
            P(PLANE, None),
        ),
        out_specs=(P(AXES, None), P(None, PLANE), P(PLANE, None)),
        check_vma=False,
    )
```

```python
import itertools
import math

import jax
import jax.numpy as jnp
from jax import lax
from jax.experimental import pallas as pl
from jax.experimental.pallas import tpu as pltpu
from jax.sharding import PartitionSpec as P

EXPERTS = 8
DRAFT = 5
CAP = 3
LEARNING_RATE = 0.5
AXES = ("y_lo", "z_pair", "z_in", "core", "x", "y_hi")
SIZES = (2, 4, 2, 2, 4, 2)
OWNERS = ("y_lo", "z_pair")
PLANE = ("y_lo", "x", "y_hi")
PARTS = (2, 8, 2, 4, 2)


def flat(place):
    index = 0
    for size, at in zip(PARTS, place):
        index = index * size + at
    return index


def permute(value, move):
    pairs = []
    for place in itertools.product(*(range(size) for size in PARTS)):
        pairs.append((flat(place), flat(move(*place))))
    return lax.ppermute(value, AXES, pairs)


def other_core(g, z, c, x, h):
    return g, z, 1 - c, x, h


def x_step(by):
    return lambda g, z, c, x, h: (g, z, c, (x + by) % 4, h)


def y_step(by):
    def move(g, z, c, x, h):
        y = (2 * h + g + by) % 4
        return y % 2, z, c, x, y // 2

    return move


def z_step(by):
    return lambda g, z, c, x, h: (g, (z + by) % 8, c, x, h)


def z_swap(g, z, c, x, h):
    return g, z ^ 1, c, x, h


def h_swap(g, z, c, x, h):
    return g, z, c, x, 1 - h


def by_core(first, second):
    return lambda g, z, c, x, h: (second if c else first)(g, z, c, x, h)


X_RING = (x_step(1), x_step(-1), x_step(1), x_step(-1), x_step(2))
X_BACK = (x_step(-1), x_step(1), x_step(-1), x_step(1), x_step(2))
Y_RING = (y_step(1), y_step(-1), y_step(1), y_step(-1), y_step(2))
Y_BACK = (y_step(-1), y_step(1), y_step(-1), y_step(1), y_step(2))
SQUARE = (z_swap, h_swap, h_swap, z_swap, lambda g, z, c, x, h: (g, z ^ 1, c, x, 1 - h))


def mixed(first, second):
    return tuple(by_core(a, b) for a, b in zip(first, second))


BLOCK_RINGS = (mixed(SQUARE, X_RING), mixed(X_RING, SQUARE))
BLOCK_BACK = (mixed(SQUARE, X_BACK), mixed(X_BACK, SQUARE))
PLANE_RINGS = (mixed(X_RING, Y_RING), mixed(Y_RING, X_RING))
PLANE_BACK = (mixed(X_BACK, Y_BACK), mixed(Y_BACK, X_BACK))
LARGE, SMALL = 20 * 1024 * 1024, 6 * 1024 * 1024
IN_VMEM = True
PACK = 3


def kernel_call(body, outs, *args, scalars=(), scratch=(), after=(), plain=(), hbm=0, limit=SMALL, flops=0):
    many = isinstance(outs, (list, tuple))
    listed = list(outs) if many else [outs]
    first, last = len(scalars), len(scalars) + len(args)
    idle = len(after)

    def run(*refs):
        body(*refs[:last], *refs[last + idle :])

    if IN_VMEM:
        plain = (*plain, *range(len(args) - hbm, len(args)))
        args = [
            pltpu.with_memory_space_constraint(a, pltpu.HBM if i in plain else pltpu.VMEM)
            for i, a in enumerate(args)
        ]
        after = [pltpu.with_memory_space_constraint(a, pltpu.VMEM) for a in after]
    size = sum(math.prod(a.shape) * jnp.dtype(a.dtype).itemsize for a in (*args, *listed))
    out = pl.pallas_call(
        run,
        out_shape=listed if many else outs,
        in_specs=[pl.BlockSpec(memory_space=pltpu.SMEM)] * first
        + [pl.BlockSpec(memory_space=pltpu.VMEM)] * (last - first - hbm)
        + [pl.BlockSpec(memory_space=pl.ANY)] * hbm
        + [pl.BlockSpec(memory_space=pltpu.VMEM)] * len(after),
        out_specs=[pl.BlockSpec(memory_space=pltpu.VMEM)] * len(listed)
        if many
        else pl.BlockSpec(memory_space=pltpu.VMEM),
        scratch_shapes=list(scratch),
        compiler_params=pltpu.CompilerParams(vmem_limit_bytes=limit),
        cost_estimate=pl.CostEstimate(flops=flops, bytes_accessed=size, transcendentals=0),
    )(*scalars, *args, *after)
    return out


def like(*shape, dtype=jnp.bfloat16):
    if IN_VMEM:
        return pltpu.VMEM(shape, dtype)
    return jax.ShapeDtypeStruct(shape, dtype)


def in_hbm(*shape, dtype=jnp.bfloat16):
    return jax.ShapeDtypeStruct(shape, dtype)


def dot(a, b, contract, precision=None):
    return lax.dot_general(
        a, b, (contract, ((), ())), precision=precision, preferred_element_type=jnp.float32
    )


NN, NT, TN = ((1,), (0,)), ((1,), (1,)), ((0,), (0,))


def f32(value):
    return value.astype(jnp.float32)


def near(value, ring):
    return [permute(value, ring[i]) for i in (0, 1, 4)]


def joined(pieces, after=()):
    n, m = pieces[0].shape

    def body(*refs):
        for i, ref in enumerate(refs[:-1]):
            refs[-1][i * n : (i + 1) * n] = ref[...]

    return kernel_call(body, like(n * len(pieces), m), *pieces, after=after)


def halves(a, b, after=()):
    n, m = a.shape
    half = m // 2

    def body(a_ref, b_ref, left, right):
        left[...], right[...] = a_ref[:, :half], b_ref[:, half:]

    return kernel_call(body, [like(n, half)] * 2, a, b, after=after)


def halves_of_sum(a, b):
    n, m = a.shape
    half = m // 2

    def body(a_ref, b_ref, left, right):
        total = (f32(a_ref[...]) + f32(b_ref[...])).astype(jnp.bfloat16)
        left[...], right[...] = total[:, :half], total[:, half:]

    return kernel_call(body, [like(n, half)] * 2, a, b)


def passed_on(a, b, left, right, after=()):
    n, m = a[0].shape
    half, count = m // 2, len(a)

    def body(*refs):
        ins, outs = refs[: 2 * count + 2], refs[2 * count + 2 :]
        for parts, far, out, where in (
            (ins[:count], ins[-2], outs[0], slice(0, half)),
            (ins[count : 2 * count], ins[-1], outs[1], slice(half, m)),
        ):
            other = slice(half, m) if where.start == 0 else slice(0, half)
            out[:, where] = (sum(f32(p[:, where]) for p in parts) + f32(far[...])).astype(
                jnp.bfloat16
            )
            out[:, other] = sum(f32(p[:, other]) for p in parts).astype(jnp.bfloat16)

    return kernel_call(body, [like(n, m)] * 2, *a, *b, left, right, after=after)


def quarters_of_sum(parts, after=()):
    n, m = parts[0].shape
    n //= 4

    def body(*refs):
        for i, out in enumerate(refs[-4:]):
            rows = slice(i * n, (i + 1) * n)
            out[...] = sum(f32(p[rows]) for p in refs[:-4]).astype(jnp.bfloat16)

    return kernel_call(body, [like(n, m)] * 4, *parts, after=after)


def brought(value, sources, after=()):
    count = len(sources)

    def body(*refs):
        out, targets, sems = refs[count + 1], refs[count + 2 : -1], refs[-1]
        copies = [
            pltpu.make_async_copy(source, target, sems.at[i])
            for i, (source, target) in enumerate(zip(refs[1 : count + 1], targets))
        ]
        for copy in copies:
            copy.start()
        out[...] = refs[0][...]
        for copy in copies:
            copy.wait()

    return kernel_call(
        body, [like(*a.shape) for a in (value, *sources)], value, *sources, after=after,
        hbm=count, scratch=[pltpu.SemaphoreType.DMA((count,))],
    )


def rows_of(pieces, after=()):
    count, width = pieces.shape[0] * CAP, pieces.shape[2]

    def body(in_ref, out_ref, wide):
        for k in range(EXPERTS):
            wide[k * CAP : (k + 1) * CAP] = f32(in_ref[k])
        out_ref[...] = wide[...].astype(jnp.bfloat16)

    return kernel_call(
        body, like(count, width), pieces, scratch=[pltpu.VMEM((count, width), jnp.float32)],
        after=after,
    )


def pieces_of_sum(parts, after=()):
    count, width = parts[0].shape

    def body(*refs):
        ins, (out_ref, wide) = refs[:-2], refs[-2:]
        wide[...] = sum(f32(p[...]) for p in ins)
        for k in range(EXPERTS):
            out_ref[k] = wide[k * CAP : (k + 1) * CAP].astype(jnp.bfloat16)

    return kernel_call(
        body, in_hbm(EXPERTS, CAP, width), *parts, after=after,
        scratch=[pltpu.VMEM((count, width), jnp.float32)],
    )


def slots(ids, lanes):
    slot = lax.broadcasted_iota(jnp.int32, (EXPERTS * CAP, lanes), 0)
    expert, place_in = slot // CAP, slot % CAP
    named = (ids[0:1] == expert) | (ids[1:2] == expert)
    at = lax.broadcasted_iota(jnp.int32, (lanes, lanes), 0)
    to = lax.broadcasted_iota(jnp.int32, (lanes, lanes), 1)
    earlier = jnp.where((at < to) & (at // 10 == to // 10), 1.0, 0.0).astype(jnp.bfloat16)
    before = dot(jnp.where(named, 1.0, 0.0).astype(jnp.bfloat16), earlier, NN)
    return jnp.where(named & (before == f32(place_in)), 1.0, 0.0), expert


def send_body(ids_ref, hidden_ref, out_ref, wide):
    taken, _ = slots(ids_ref[...], hidden_ref.shape[0])
    wide[...] = dot(taken.astype(jnp.bfloat16), hidden_ref[...], NN)
    for k in range(EXPERTS):
        out_ref[k] = wide[k * CAP : (k + 1) * CAP].astype(jnp.bfloat16)


def pack_body(accept_ref, hidden_ref, packed_ref):
    rows, width = hidden_ref.shape
    part = width // PACK
    to = lax.broadcasted_iota(jnp.int32, (32, rows), 0)
    row = lax.broadcasted_iota(jnp.int32, (32, rows), 1)
    keep = jnp.zeros((32, rows), jnp.float32)
    for i in range(rows // DRAFT):
        kept = (row // DRAFT == i) & (row % DRAFT >= accept_ref[i])
        keep += jnp.where(kept, 1.0, 0.0)
    count = jnp.sum(keep[:1])
    total = jnp.where(lax.broadcasted_iota(jnp.int32, (32, part), 0) == 30, count, 0.0)
    for j in range(PACK):
        pick = jnp.where(to == row + 10 * j, keep, 0.0).astype(jnp.bfloat16)
        total += dot(pick, hidden_ref[:, j * part : (j + 1) * part], NN)
    packed_ref[...] = total.astype(jnp.bfloat16)


def combine_body(ids_ref, logit_ref, keep_ref, hidden_ref, *refs):
    guess, (returned_ref, verified_ref, slope_ref, wide) = refs[:4], refs[4:]
    rows, width = hidden_ref.shape
    part = width // PACK
    for k in range(EXPERTS):
        wide[k * CAP : (k + 1) * CAP] = f32(returned_ref[k])
    ids = ids_ref[...]
    taken, expert = slots(ids, 32)
    zero, one = logit_ref[0:1], logit_ref[1:2]
    first, second = 1.0 / (1.0 + jnp.exp(one - zero)), 1.0 / (1.0 + jnp.exp(zero - one))
    gated = taken * jnp.where(ids[0:1] == expert, first, second)
    combined = dot(gated[:, :rows], wide[...], TN, lax.Precision.HIGHEST)
    verified_ref[...] = (f32(hidden_ref[...]) + combined).astype(jnp.bfloat16)
    lane = lax.broadcasted_iota(jnp.int32, gated.shape, 1)
    kept = gated * keep_ref[...]
    teacher = jnp.zeros((32, part), jnp.float32)
    for j in range(PACK):
        table = jnp.where((lane >= 10 * j) & (lane < 10 * j + 10), kept, 0.0)
        teacher += dot(table, wide[:, j * part : (j + 1) * part], TN, lax.Precision.HIGHEST)
    teacher = f32(teacher.astype(jnp.bfloat16))
    slope_ref[...] = (sum(f32(g[...]) for g in guess) - teacher).astype(jnp.bfloat16)


def expert_rows(blocks, w_gate, w_up, w_down, after=()):
    width = w_gate.shape[0]
    heights = [block[0].shape[0] for block in blocks]
    flat_blocks = [part for block in blocks for part in block]
    total, count = sum(heights), len(flat_blocks)
    step = width // 6

    def body(*refs):
        ins, (gate_ref, up_ref, down_ref) = list(refs[:count]), refs[count : count + 3]
        outs, rows = refs[count + 3 : -1], refs[-1]
        at = 0
        for block, height in zip(blocks, heights):
            column = 0
            for _ in block:
                ref = ins.pop(0)
                rows[at : at + height, column : column + ref.shape[1]] = ref[...]
                column += ref.shape[1]
            at += height
        gate = dot(rows[...], gate_ref[...], NN)
        upper = dot(rows[...], up_ref[...], NN)
        acts = (gate / (1.0 + jnp.exp(-gate)) * upper).astype(jnp.bfloat16)
        for i in range(6):
            columns = slice(i * step, (i + 1) * step)
            out = dot(acts, down_ref[:, columns], NN).astype(jnp.bfloat16)
            at = 0
            for ref, height in zip(outs, heights):
                ref[:, columns] = out[at : at + height]
                at += height

    return kernel_call(
        body, [like(height, width) for height in heights], *flat_blocks, w_gate, w_up, w_down,
        scratch=[pltpu.VMEM((total, width), jnp.bfloat16)], after=after, limit=LARGE,
        flops=6 * total * width * w_gate.shape[1],
    )


def shifted(value, by):
    return pltpu.roll(value, by % value.shape[0], 0) if by else value


def fill(target, pieces):
    n = pieces[0].shape[0]
    for i, ref in enumerate(pieces):
        target[i * n : (i + 1) * n] = ref[...]


def stacked(target, source):
    units, part = source.shape[0], target.shape[1]
    for j in range(PACK):
        target[j * units : (j + 1) * units] = source[:, j * part : (j + 1) * part]


def spread_rows(value):
    return jnp.concatenate([shifted(value, 10 * j) for j in range(PACK)], axis=1).astype(
        jnp.bfloat16
    )


def gathered_rows(value, units):
    total = sum(shifted(value[:, j * units : (j + 1) * units], -10 * j) for j in range(PACK))
    row = lax.broadcasted_iota(jnp.int32, total.shape, 0) % 32
    return jnp.where(row < 10, total, 0.0)


def forward_body(*refs):
    pieces, (in_ref, out_ref), (x_ref, inner_ref, *guesses) = refs[:4], refs[4:6], refs[6:-2]
    in_rows, out_rows = refs[-2:]
    fill(x_ref, pieces)
    stacked(in_rows, in_ref)
    stacked(out_rows, out_ref)
    rows, part = x_ref.shape
    inner = gathered_rows(dot(x_ref[...], in_rows[...], NT), inner_ref.shape[1])
    inner_ref[...] = inner
    active = spread_rows(inner / (1.0 + jnp.exp(-inner)))
    guess = dot(active, out_rows[...], NN).astype(jnp.bfloat16)
    n, half = rows // 4, part // 2
    for i in range(3):
        guesses[i][...] = guess[i * n : (i + 1) * n]
    guesses[3][...], guesses[4][...] = guess[3 * n :, :half], guess[3 * n :, half:]


def put(ref, left, right):
    piece = ref.shape[2]
    grad = dot(spread_rows(left), right[...], TN).astype(jnp.bfloat16)
    for i in range(8):
        ref[i, : grad.shape[0], :] = grad[:, i * piece : (i + 1) * piece]


def gradient(pieces, x, inner, draft_out, core, of_in):
    units, part = inner.shape[1], x.shape[1]
    piece = part // 8

    def body(core_ref, *refs):
        blocks, (x_ref, inner_ref, out_ref, grad_ref, slope, out_rows) = refs[:4], refs[4:]
        fill(slope, blocks)
        inner = inner_ref[...]
        sigma = 1.0 / (1.0 + jnp.exp(-inner))
        line = lax.broadcasted_iota(jnp.int32, (x.shape[0], piece), 0) % 32
        count = jnp.sum(jnp.where(line == 30, f32(x_ref[:, :piece]), 0.0), axis=0, keepdims=True)
        high = jnp.floor(count * 0.0625)
        line = lax.broadcasted_iota(jnp.int32, (8, piece), 0)
        tail = jnp.where(line == 0, high, jnp.where(line == 1, count - 16.0 * high, 0.0))
        for i in range(8):
            grad_ref[i, PACK * units :, :] = tail.astype(jnp.bfloat16)

        @pl.when(core_ref[0] == of_in)
        def _():
            stacked(out_rows, out_ref)
            back = gathered_rows(dot(slope[...], out_rows[...], NT), units)
            put(grad_ref, back * sigma * (1.0 + inner * (1.0 - sigma)), x_ref)

        @pl.when(core_ref[0] != of_in)
        def _():
            put(grad_ref, inner * sigma, slope)

    return kernel_call(
        body, like(8, PACK * units + 8, piece), *pieces, x, inner, draft_out, scalars=(core,),
        scratch=[
            pltpu.VMEM(x.shape, jnp.bfloat16), pltpu.VMEM((PACK * units, part), jnp.bfloat16)
        ],
        plain=(5,), limit=LARGE,
    )


def place_of(z_ref, core_ref, k):
    return (z_ref[0] + 8 + k * (1 - 2 * core_ref[0])) % 8


def turn_body(core_ref, z_ref, mine_ref, other_ref, *outs):
    for k, out in enumerate(outs):
        at = place_of(z_ref, core_ref, k)
        out[...] = (f32(mine_ref[at]) + f32(other_ref[at])).astype(jnp.bfloat16)


def update_body(core_ref, z_ref, *refs):
    pieces, (in_ref, out_ref), new_ref = refs[:8], refs[8:10], refs[10]
    total = pieces[0][...].astype(jnp.float32)
    for ref in pieces[1:]:
        total += ref[...].astype(jnp.float32)
    rows, piece = new_ref.shape
    units, part = rows // PACK, in_ref.shape[1] // PACK
    rejected = 16.0 * total[rows : rows + 1] + total[rows + 1 : rows + 2]
    rate = (2.0 * LEARNING_RATE) / rejected
    in_core = jnp.full((units, piece), core_ref[0], jnp.int32) == 0
    for j in range(PACK):
        columns = pl.ds(pl.multiple_of(j * part + z_ref[0] * piece, piece), piece)
        old = jnp.where(
            in_core, in_ref[:, columns].astype(jnp.float32), out_ref[:, columns].astype(jnp.float32)
        )
        new = old - rate * total[j * units : (j + 1) * units]
        new_ref[j * units : (j + 1) * units] = new.astype(jnp.bfloat16)


def spread_body(core_ref, z_ref, *refs):
    pieces, out_ref = refs[:8], refs[8]
    rows, piece = pieces[0].shape
    units, part = rows // PACK, out_ref.shape[1] // PACK
    for k, ref in enumerate(pieces):
        at = place_of(z_ref, core_ref, -k)
        for j in range(PACK):
            columns = pl.ds(pl.multiple_of(j * part + at * piece, piece), piece)
            out_ref[:, columns] = ref[j * units : (j + 1) * units]


def per_device(
    hidden, expert_ids, gate_logits, accept_len, w_gate, w_up, w_down, draft_in, draft_out
):
    local_rows, width = hidden.shape
    part, units = width // PACK, draft_out.shape[0]
    core = lax.axis_index("core").astype(jnp.int32).reshape(1)
    z = (2 * lax.axis_index("z_pair") + lax.axis_index("z_in")).astype(jnp.int32).reshape(1)

    def lanes(rows, empty):
        return jnp.pad(jnp.tile(rows, (1, PACK)), ((0, 0), (0, 2)), constant_values=empty)

    keep = jnp.arange(local_rows, dtype=jnp.int32) % DRAFT >= jnp.repeat(accept_len, DRAFT)
    keep = lanes(f32(keep)[None], 0.0)
    ids = lanes(expert_ids.T, EXPERTS)
    logits = lanes(gate_logits.T, 0.0)
    wide = pltpu.VMEM((EXPERTS * CAP, width), jnp.float32)

    weights = (w_gate, w_up, w_down)
    outgoing = kernel_call(
        send_body, in_hbm(EXPERTS, CAP, width), expert_ids.T, hidden, scratch=[wide],
        plain=(0, 1), flops=2 * 24 * 10 * width,
    )
    packed = kernel_call(
        pack_body, like(32, part), hidden, scalars=(accept_len,), plain=(0,),
        flops=2 * 32 * 10 * width,
    )

    def exchange(pieces):
        return lax.all_to_all(pieces, OWNERS, split_axis=0, concat_axis=0, tiled=True)

    inputs = [packed, *near(packed, PLANE_RINGS[0])]
    own = rows_of(exchange(outgoing), after=inputs)
    inputs = joined(inputs)
    in_a, in_b = [permute(inputs, move) for move in PLANE_RINGS[1][:2]]
    near_own = near(own, BLOCK_RINGS[0])

    block = joined([own, *near_own], after=[in_a, in_b])
    a, b = [permute(block, move) for move in BLOCK_RINGS[1][:2]]
    again, *weights = brought(inputs, weights, after=[block])
    in_far = permute(again, PLANE_RINGS[1][4])
    left, right = halves(a, b, after=[in_far])
    left, right = permute(left, BLOCK_RINGS[1][2]), permute(right, BLOCK_RINGS[1][3])
    a_t, b_t, a_o, b_o = expert_rows(
        [[a], [b], [permute(a, other_core)], [permute(b, other_core)]], *weights
    )
    far_t, far_o = expert_rows(
        [[left, right], [permute(left, other_core), permute(right, other_core)]],
        *weights, after=[a_t],
    )

    left, right = halves_of_sum(far_t, permute(far_o, other_core))
    left, right = permute(left, BLOCK_BACK[1][2]), permute(right, BLOCK_BACK[1][3])
    block_t, block_o = expert_rows(
        [[block], [permute(block, other_core)]], *weights, after=[far_t]
    )
    x, inner, *guess = kernel_call(
        forward_body,
        [like(512, part), like(512, units, dtype=jnp.float32)]
        + [like(128, part)] * 3 + [like(128, part // 2)] * 2,
        inputs, in_a, in_b, in_far, draft_in.T, draft_out,
        after=[far_t], limit=LARGE, flops=12 * 512 * part * units,
        scratch=[pltpu.VMEM((PACK * units, part), jnp.bfloat16)] * 2,
    )
    a, b = passed_on(
        [a_t, permute(a_o, other_core)], [b_t, permute(b_o, other_core)], left, right, after=[guess[0]]
    )
    guess_left, guess_right = permute(guess[3], PLANE_BACK[1][2]), permute(guess[4], PLANE_BACK[1][3])
    a, b = permute(a, BLOCK_BACK[1][0]), permute(b, BLOCK_BACK[1][1])
    block = quarters_of_sum([block_t, permute(block_o, other_core), a, b])
    guess_a, guess_b = passed_on(
        guess[1:2], guess[2:3], guess_left, guess_right, after=[block[0]]
    )
    guess_a, guess_b = permute(guess_a, PLANE_BACK[1][0]), permute(guess_b, PLANE_BACK[1][1])
    summed = pieces_of_sum(
        [block[0]] + [permute(block[i], BLOCK_BACK[0][(0, 1, 4)[i - 1]]) for i in (1, 2, 3)],
    )
    guess = quarters_of_sum([guess[0], guess_a, guess_b], after=[summed])
    guess = [guess[0]] + [permute(guess[i], PLANE_BACK[0][(0, 1, 4)[i - 1]]) for i in (1, 2, 3)]

    verified, slope = kernel_call(
        combine_body,
        [in_hbm(local_rows, width), like(32, part)],
        ids, logits, keep, hidden, *guess, exchange(summed), scratch=[wide],
    )

    slope = joined([slope, *near(slope, PLANE_RINGS[0])])
    slope = [slope, *near(slope, PLANE_RINGS[1])]
    other = permute(gradient(slope, x, inner, draft_out, core, 1), other_core)
    mine = gradient(slope, x, inner, draft_out, core, 0)

    order = (4, 3, 5, 2, 6, 1, 7)

    def around(pieces):
        moved = {0: pieces[0]}
        for k in order:
            moved[k] = permute(pieces[k], by_core(z_step(k), z_step(-k)))
        return [moved[k] for k in range(8)]

    turned = kernel_call(turn_body, [like(*mine.shape[1:])] * 8, mine, other, scalars=(core, z))
    new = kernel_call(
        update_body, like(PACK * units, part // 8), *around(turned), draft_in.T, draft_out,
        scalars=(core, z),
    )
    gathered = kernel_call(
        spread_body, like(units, width), *around([new] * 8), scalars=(core, z)
    )
    other = permute(gathered, other_core)
    in_core = core[0] == 0
    new_in = jnp.where(in_core, gathered, other).T
    new_out = jnp.where(in_core, other, gathered)
    return (verified, new_in, new_out)


def solution(mesh):
    return jax.shard_map(
        per_device,
        mesh=jax.sharding.Mesh(mesh.devices.reshape(SIZES), AXES),
        in_specs=(
            P(AXES, None),
            P(AXES, None),
            P(AXES, None),
            P(AXES),
            P(None, AXES),
            P(None, AXES),
            P(AXES, None),
            P(None, PLANE),
            P(PLANE, None),
        ),
        out_specs=(P(AXES, None), P(None, PLANE), P(PLANE, None)),
        check_vma=False,
    )
```

```python
import itertools
import math

import jax
import jax.numpy as jnp
from jax import lax
from jax.experimental import pallas as pl
from jax.experimental.pallas import tpu as pltpu
from jax.sharding import PartitionSpec as P

EXPERTS = 8
DRAFT = 5
CAP = 3
LEARNING_RATE = 0.5
AXES = ("y_lo", "z_pair", "z_in", "core", "x", "y_hi")
SIZES = (2, 4, 2, 2, 4, 2)
OWNERS = ("y_lo", "z_pair")
PLANE = ("y_lo", "x", "y_hi")
PARTS = (2, 8, 2, 4, 2)


def flat(place):
    index = 0
    for size, at in zip(PARTS, place):
        index = index * size + at
    return index


def permute(value, move):
    pairs = []
    for place in itertools.product(*(range(size) for size in PARTS)):
        pairs.append((flat(place), flat(move(*place))))
    return lax.ppermute(value, AXES, pairs)


def other_core(g, z, c, x, h):
    return g, z, 1 - c, x, h


def x_step(by):
    return lambda g, z, c, x, h: (g, z, c, (x + by) % 4, h)


def y_step(by):
    def move(g, z, c, x, h):
        y = (2 * h + g + by) % 4
        return y % 2, z, c, x, y // 2

    return move


def z_step(by):
    return lambda g, z, c, x, h: (g, (z + by) % 8, c, x, h)


def z_swap(g, z, c, x, h):
    return g, z ^ 1, c, x, h


def h_swap(g, z, c, x, h):
    return g, z, c, x, 1 - h


def by_core(first, second):
    return lambda g, z, c, x, h: (second if c else first)(g, z, c, x, h)


X_RING = (x_step(1), x_step(-1), x_step(1), x_step(-1), x_step(2))
X_BACK = (x_step(-1), x_step(1), x_step(-1), x_step(1), x_step(2))
Y_RING = (y_step(1), y_step(-1), y_step(1), y_step(-1), y_step(2))
Y_BACK = (y_step(-1), y_step(1), y_step(-1), y_step(1), y_step(2))
SQUARE = (z_swap, h_swap, h_swap, z_swap, lambda g, z, c, x, h: (g, z ^ 1, c, x, 1 - h))


def mixed(first, second):
    return tuple(by_core(a, b) for a, b in zip(first, second))


BLOCK_RINGS = (mixed(SQUARE, X_RING), mixed(X_RING, SQUARE))
BLOCK_BACK = (mixed(SQUARE, X_BACK), mixed(X_BACK, SQUARE))
PLANE_RINGS = (mixed(X_RING, Y_RING), mixed(Y_RING, X_RING))
PLANE_BACK = (mixed(X_BACK, Y_BACK), mixed(Y_BACK, X_BACK))
LARGE, SMALL = 20 * 1024 * 1024, 6 * 1024 * 1024
IN_VMEM = True
Z_ORDER = (0, 2, 6, 4, 1, 7, 3, 5)
PACK = 3


def kernel_call(body, outs, *args, scalars=(), scratch=(), after=(), plain=(), hbm=0, limit=SMALL, flops=0):
    many = isinstance(outs, (list, tuple))
    listed = list(outs) if many else [outs]
    first, last = len(scalars), len(scalars) + len(args)
    idle = len(after)

    def run(*refs):
        body(*refs[:last], *refs[last + idle :])

    if IN_VMEM:
        plain = (*plain, *range(len(args) - hbm, len(args)))
        args = [
            pltpu.with_memory_space_constraint(a, pltpu.HBM if i in plain else pltpu.VMEM)
            for i, a in enumerate(args)
        ]
        after = [pltpu.with_memory_space_constraint(a, pltpu.VMEM) for a in after]
    size = sum(math.prod(a.shape) * jnp.dtype(a.dtype).itemsize for a in (*args, *listed))
    out = pl.pallas_call(
        run,
        out_shape=listed if many else outs,
        in_specs=[pl.BlockSpec(memory_space=pltpu.SMEM)] * first
        + [pl.BlockSpec(memory_space=pltpu.VMEM)] * (last - first - hbm)
        + [pl.BlockSpec(memory_space=pl.ANY)] * hbm
        + [pl.BlockSpec(memory_space=pltpu.VMEM)] * len(after),
        out_specs=[pl.BlockSpec(memory_space=pltpu.VMEM)] * len(listed)
        if many
        else pl.BlockSpec(memory_space=pltpu.VMEM),
        scratch_shapes=list(scratch),
        compiler_params=pltpu.CompilerParams(vmem_limit_bytes=limit),
        cost_estimate=pl.CostEstimate(flops=flops, bytes_accessed=size, transcendentals=0),
    )(*scalars, *args, *after)
    return out


def like(*shape, dtype=jnp.bfloat16):
    if IN_VMEM:
        return pltpu.VMEM(shape, dtype)
    return jax.ShapeDtypeStruct(shape, dtype)


def in_hbm(*shape, dtype=jnp.bfloat16):
    return jax.ShapeDtypeStruct(shape, dtype)


def dot(a, b, contract, precision=None):
    return lax.dot_general(
        a, b, (contract, ((), ())), precision=precision, preferred_element_type=jnp.float32
    )


NN, NT, TN = ((1,), (0,)), ((1,), (1,)), ((0,), (0,))


def f32(value):
    return value.astype(jnp.float32)


def near(value, ring):
    return [permute(value, ring[i]) for i in (0, 1, 4)]


def joined(pieces, after=(), order=(0, 1, 2, 3)):
    n, m = pieces[0].shape

    def body(*refs):
        for i, ref in zip(order, refs[:-1]):
            refs[-1][i * n : (i + 1) * n] = ref[...]

    return kernel_call(
        body, like(n * len(pieces), m), *[pieces[i] for i in order], after=after
    )


def halves(a, b, after=()):
    n, m = a.shape
    half = m // 2

    def body(a_ref, b_ref, left, right):
        left[...], right[...] = a_ref[:, :half], b_ref[:, half:]

    return kernel_call(body, [like(n, half)] * 2, a, b, after=after)


def halves_of_sum(a, b):
    n, m = a.shape
    half = m // 2

    def body(a_ref, b_ref, left, right):
        total = (f32(a_ref[...]) + f32(b_ref[...])).astype(jnp.bfloat16)
        left[...], right[...] = total[:, :half], total[:, half:]

    return kernel_call(body, [like(n, half)] * 2, a, b)


def passed_on(a, b, left, right, after=()):
    n, m = a[0].shape
    half, count = m // 2, len(a)

    def body(*refs):
        ins, outs = refs[: 2 * count + 2], refs[2 * count + 2 :]
        for parts, far, out, where in (
            (ins[:count], ins[-2], outs[0], slice(0, half)),
            (ins[count : 2 * count], ins[-1], outs[1], slice(half, m)),
        ):
            other = slice(half, m) if where.start == 0 else slice(0, half)
            out[:, where] = (sum(f32(p[:, where]) for p in parts) + f32(far[...])).astype(
                jnp.bfloat16
            )
            out[:, other] = sum(f32(p[:, other]) for p in parts).astype(jnp.bfloat16)

    return kernel_call(body, [like(n, m)] * 2, *a, *b, left, right, after=after)


def quarters_of_sum(parts, after=()):
    n, m = parts[0].shape
    n //= 4

    def body(*refs):
        for i, out in enumerate(refs[-4:]):
            rows = slice(i * n, (i + 1) * n)
            out[...] = sum(f32(p[rows]) for p in refs[:-4]).astype(jnp.bfloat16)

    return kernel_call(body, [like(n, m)] * 4, *parts, after=after)


def brought(value, sources, after=()):
    count = len(sources)

    def body(*refs):
        out, targets, sems = refs[count + 1], refs[count + 2 : -1], refs[-1]
        copies = [
            pltpu.make_async_copy(source, target, sems.at[i])
            for i, (source, target) in enumerate(zip(refs[1 : count + 1], targets))
        ]
        for copy in copies:
            copy.start()
        out[...] = refs[0][...]
        for copy in copies:
            copy.wait()

    return kernel_call(
        body, [like(*a.shape) for a in (value, *sources)], value, *sources, after=after,
        hbm=count, scratch=[pltpu.SemaphoreType.DMA((count,))],
    )


def rows_of(pieces, after=()):
    count, width = pieces.shape[0] * CAP, pieces.shape[2]

    def body(in_ref, out_ref, wide):
        for k in range(EXPERTS):
            wide[k * CAP : (k + 1) * CAP] = f32(in_ref[k])
        out_ref[...] = wide[...].astype(jnp.bfloat16)

    return kernel_call(
        body, like(count, width), pieces, scratch=[pltpu.VMEM((count, width), jnp.float32)],
        after=after,
    )


def pieces_of_sum(parts, after=()):
    count, width = parts[0].shape

    def body(*refs):
        ins, (out_ref, wide) = refs[:-2], refs[-2:]
        wide[...] = sum(f32(p[...]) for p in ins)
        for k in range(EXPERTS):
            out_ref[k] = wide[k * CAP : (k + 1) * CAP].astype(jnp.bfloat16)

    return kernel_call(
        body, in_hbm(EXPERTS, CAP, width), *parts, after=after,
        scratch=[pltpu.VMEM((count, width), jnp.float32)],
    )


def slots(ids, lanes):
    slot = lax.broadcasted_iota(jnp.int32, (EXPERTS * CAP, lanes), 0)
    expert, place_in = slot // CAP, slot % CAP
    named = (ids[0:1] == expert) | (ids[1:2] == expert)
    at = lax.broadcasted_iota(jnp.int32, (lanes, lanes), 0)
    to = lax.broadcasted_iota(jnp.int32, (lanes, lanes), 1)
    earlier = jnp.where((at < to) & (at // 10 == to // 10), 1.0, 0.0).astype(jnp.bfloat16)
    before = dot(jnp.where(named, 1.0, 0.0).astype(jnp.bfloat16), earlier, NN)
    return jnp.where(named & (before == f32(place_in)), 1.0, 0.0), expert


def send_body(ids_ref, hidden_ref, out_ref, wide):
    taken, _ = slots(ids_ref[...], hidden_ref.shape[0])
    wide[...] = dot(taken.astype(jnp.bfloat16), hidden_ref[...], NN)
    for k in range(EXPERTS):
        out_ref[k] = wide[k * CAP : (k + 1) * CAP].astype(jnp.bfloat16)


def pack_body(accept_ref, hidden_ref, packed_ref):
    rows, width = hidden_ref.shape
    part = width // PACK
    to = lax.broadcasted_iota(jnp.int32, (32, rows), 0)
    row = lax.broadcasted_iota(jnp.int32, (32, rows), 1)
    keep = jnp.zeros((32, rows), jnp.float32)
    for i in range(rows // DRAFT):
        kept = (row // DRAFT == i) & (row % DRAFT >= accept_ref[i])
        keep += jnp.where(kept, 1.0, 0.0)
    count = jnp.sum(keep[:1])
    total = jnp.where(lax.broadcasted_iota(jnp.int32, (32, part), 0) == 30, count, 0.0)
    for j in range(PACK):
        pick = jnp.where(to == row + 10 * j, keep, 0.0).astype(jnp.bfloat16)
        total += dot(pick, hidden_ref[:, j * part : (j + 1) * part], NN)
    packed_ref[...] = total.astype(jnp.bfloat16)


def combine_body(ids_ref, logit_ref, keep_ref, hidden_ref, *refs):
    guess, (returned_ref, verified_ref, slope_ref, wide) = refs[:4], refs[4:]
    rows, width = hidden_ref.shape
    part = width // PACK
    for k in range(EXPERTS):
        wide[k * CAP : (k + 1) * CAP] = f32(returned_ref[k])
    ids = ids_ref[...]
    taken, expert = slots(ids, 32)
    zero, one = logit_ref[0:1], logit_ref[1:2]
    first, second = 1.0 / (1.0 + jnp.exp(one - zero)), 1.0 / (1.0 + jnp.exp(zero - one))
    gated = taken * jnp.where(ids[0:1] == expert, first, second)
    combined = dot(gated[:, :rows], wide[...], TN, lax.Precision.HIGHEST)
    verified_ref[...] = (f32(hidden_ref[...]) + combined).astype(jnp.bfloat16)
    lane = lax.broadcasted_iota(jnp.int32, gated.shape, 1)
    kept = gated * keep_ref[...]
    teacher = jnp.zeros((32, part), jnp.float32)
    for j in range(PACK):
        table = jnp.where((lane >= 10 * j) & (lane < 10 * j + 10), kept, 0.0)
        teacher += dot(table, wide[:, j * part : (j + 1) * part], TN, lax.Precision.HIGHEST)
    teacher = f32(teacher.astype(jnp.bfloat16))
    slope_ref[...] = (sum(f32(g[...]) for g in guess) - teacher).astype(jnp.bfloat16)


def expert_rows(blocks, w_gate, w_up, w_down, after=()):
    width = w_gate.shape[0]
    heights = [block[0].shape[0] for block in blocks]
    flat_blocks = [part for block in blocks for part in block]
    total, count = sum(heights), len(flat_blocks)
    step = width // 6

    def body(*refs):
        ins, (gate_ref, up_ref, down_ref) = list(refs[:count]), refs[count : count + 3]
        outs, rows = refs[count + 3 : -1], refs[-1]
        at = 0
        for block, height in zip(blocks, heights):
            column = 0
            for _ in block:
                ref = ins.pop(0)
                rows[at : at + height, column : column + ref.shape[1]] = ref[...]
                column += ref.shape[1]
            at += height
        gate = dot(rows[...], gate_ref[...], NN)
        upper = dot(rows[...], up_ref[...], NN)
        acts = (gate / (1.0 + jnp.exp(-gate)) * upper).astype(jnp.bfloat16)
        for i in range(6):
            columns = slice(i * step, (i + 1) * step)
            out = dot(acts, down_ref[:, columns], NN).astype(jnp.bfloat16)
            at = 0
            for ref, height in zip(outs, heights):
                ref[:, columns] = out[at : at + height]
                at += height

    return kernel_call(
        body, [like(height, width) for height in heights], *flat_blocks, w_gate, w_up, w_down,
        scratch=[pltpu.VMEM((total, width), jnp.bfloat16)], after=after, limit=LARGE,
        flops=6 * total * width * w_gate.shape[1],
    )


def shifted(value, by):
    return pltpu.roll(value, by % value.shape[0], 0) if by else value


def fill(target, pieces):
    n = pieces[0].shape[0]
    for i, ref in enumerate(pieces):
        target[i * n : (i + 1) * n] = ref[...]


def stacked(target, source):
    units, part = source.shape[0], target.shape[1]
    for j in range(PACK):
        target[j * units : (j + 1) * units] = source[:, j * part : (j + 1) * part]


def spread_rows(value):
    return jnp.concatenate([shifted(value, 10 * j) for j in range(PACK)], axis=1).astype(
        jnp.bfloat16
    )


def gathered_rows(value, units):
    total = sum(shifted(value[:, j * units : (j + 1) * units], -10 * j) for j in range(PACK))
    row = lax.broadcasted_iota(jnp.int32, total.shape, 0) % 32
    return jnp.where(row < 10, total, 0.0)


def forward_body(*refs):
    pieces, (in_ref, out_ref), (x_ref, inner_ref, *guesses) = refs[:4], refs[4:6], refs[6:-2]
    in_rows, out_rows = refs[-2:]
    fill(x_ref, pieces)
    stacked(in_rows, in_ref)
    stacked(out_rows, out_ref)
    rows, part = x_ref.shape
    inner = gathered_rows(dot(x_ref[...], in_rows[...], NT), inner_ref.shape[1])
    inner_ref[...] = inner
    active = spread_rows(inner / (1.0 + jnp.exp(-inner)))
    guess = dot(active, out_rows[...], NN).astype(jnp.bfloat16)
    n, half = rows // 4, part // 2
    for i in range(3):
        guesses[i][...] = guess[i * n : (i + 1) * n]
    guesses[3][...], guesses[4][...] = guess[3 * n :, :half], guess[3 * n :, half:]


def put(ref, left, right):
    piece = ref.shape[2]
    grad = dot(spread_rows(left), right[...], TN).astype(jnp.bfloat16)
    for i in range(8):
        ref[i, : grad.shape[0], :] = grad[:, i * piece : (i + 1) * piece]


def gradient(pieces, x, inner, draft_out, core, of_in):
    units, part = inner.shape[1], x.shape[1]
    piece = part // 8

    def body(core_ref, *refs):
        blocks, (x_ref, inner_ref, out_ref, grad_ref, slope, out_rows) = refs[:4], refs[4:]
        fill(slope, blocks)
        inner = inner_ref[...]
        sigma = 1.0 / (1.0 + jnp.exp(-inner))
        line = lax.broadcasted_iota(jnp.int32, (x.shape[0], piece), 0) % 32
        count = jnp.sum(jnp.where(line == 30, f32(x_ref[:, :piece]), 0.0), axis=0, keepdims=True)
        high = jnp.floor(count * 0.0625)
        line = lax.broadcasted_iota(jnp.int32, (8, piece), 0)
        tail = jnp.where(line == 0, high, jnp.where(line == 1, count - 16.0 * high, 0.0))
        for i in range(8):
            grad_ref[i, PACK * units :, :] = tail.astype(jnp.bfloat16)

        @pl.when(core_ref[0] == of_in)
        def _():
            stacked(out_rows, out_ref)
            back = gathered_rows(dot(slope[...], out_rows[...], NT), units)
            put(grad_ref, back * sigma * (1.0 + inner * (1.0 - sigma)), x_ref)

        @pl.when(core_ref[0] != of_in)
        def _():
            put(grad_ref, inner * sigma, slope)

    return kernel_call(
        body, like(8, PACK * units + 8, piece), *pieces, x, inner, draft_out, scalars=(core,),
        scratch=[
            pltpu.VMEM(x.shape, jnp.bfloat16), pltpu.VMEM((PACK * units, part), jnp.bfloat16)
        ],
        plain=(5,), limit=LARGE,
    )


def place_of(z_ref, core_ref, k):
    return (z_ref[0] + 8 + k * (1 - 2 * core_ref[0])) % 8


def turn_body(core_ref, z_ref, mine_ref, other_ref, *outs):
    for k, out in enumerate(outs):
        at = place_of(z_ref, core_ref, k)
        out[...] = (f32(mine_ref[at]) + f32(other_ref[at])).astype(jnp.bfloat16)


def update_body(core_ref, z_ref, *refs):
    pieces, (in_ref, out_ref), new_ref = refs[:8], refs[8:10], refs[10]
    total = pieces[0][...].astype(jnp.float32)
    for ref in pieces[1:]:
        total += ref[...].astype(jnp.float32)
    rows, piece = new_ref.shape
    units, part = rows // PACK, in_ref.shape[1] // PACK
    rejected = 16.0 * total[rows : rows + 1] + total[rows + 1 : rows + 2]
    rate = (2.0 * LEARNING_RATE) / rejected
    in_core = jnp.full((units, piece), core_ref[0], jnp.int32) == 0
    for j in range(PACK):
        columns = pl.ds(pl.multiple_of(j * part + z_ref[0] * piece, piece), piece)
        old = jnp.where(
            in_core, in_ref[:, columns].astype(jnp.float32), out_ref[:, columns].astype(jnp.float32)
        )
        new = old - rate * total[j * units : (j + 1) * units]
        new_ref[j * units : (j + 1) * units] = new.astype(jnp.bfloat16)


def spread_body(core_ref, z_ref, *refs):
    pieces, out_ref = refs[:8], refs[8]
    rows, piece = pieces[0].shape
    units, part = rows // PACK, out_ref.shape[1] // PACK
    for k, ref in zip(Z_ORDER, pieces):
        at = place_of(z_ref, core_ref, -k)
        for j in range(PACK):
            columns = pl.ds(pl.multiple_of(j * part + at * piece, piece), piece)
            out_ref[:, columns] = ref[j * units : (j + 1) * units]


def per_device(
    hidden, expert_ids, gate_logits, accept_len, w_gate, w_up, w_down, draft_in, draft_out
):
    local_rows, width = hidden.shape
    part, units = width // PACK, draft_out.shape[0]
    core = lax.axis_index("core").astype(jnp.int32).reshape(1)
    z = (2 * lax.axis_index("z_pair") + lax.axis_index("z_in")).astype(jnp.int32).reshape(1)

    def lanes(rows, empty):
        return jnp.pad(jnp.tile(rows, (1, PACK)), ((0, 0), (0, 2)), constant_values=empty)

    keep = jnp.arange(local_rows, dtype=jnp.int32) % DRAFT >= jnp.repeat(accept_len, DRAFT)
    keep = lanes(f32(keep)[None], 0.0)
    ids = lanes(expert_ids.T, EXPERTS)
    logits = lanes(gate_logits.T, 0.0)
    wide = pltpu.VMEM((EXPERTS * CAP, width), jnp.float32)

    weights = (w_gate, w_up, w_down)
    outgoing = kernel_call(
        send_body, in_hbm(EXPERTS, CAP, width), expert_ids.T, hidden, scratch=[wide],
        plain=(0, 1), flops=2 * 24 * 10 * width,
    )
    packed = kernel_call(
        pack_body, like(32, part), hidden, scalars=(accept_len,), plain=(0,),
        flops=2 * 32 * 10 * width,
    )

    def exchange(pieces):
        return lax.all_to_all(pieces, OWNERS, split_axis=0, concat_axis=0, tiled=True)

    inputs = [packed, *near(packed, PLANE_RINGS[0])]
    own = rows_of(exchange(outgoing), after=inputs)
    inputs = joined(inputs)
    in_a, in_b = [permute(inputs, move) for move in PLANE_RINGS[1][:2]]
    near_own = near(own, BLOCK_RINGS[0])

    block = joined([own, *near_own], after=[in_a, in_b])
    a, b = [permute(block, move) for move in BLOCK_RINGS[1][:2]]
    again, *weights = brought(inputs, weights, after=[block])
    in_far = permute(again, PLANE_RINGS[1][4])
    left, right = halves(a, b, after=[in_far])
    left, right = permute(left, BLOCK_RINGS[1][2]), permute(right, BLOCK_RINGS[1][3])
    a_t, b_t, a_o, b_o = expert_rows(
        [[a], [b], [permute(a, other_core)], [permute(b, other_core)]], *weights
    )
    far_t, far_o = expert_rows(
        [[left, right], [permute(left, other_core), permute(right, other_core)]],
        *weights, after=[a_t],
    )

    left, right = halves_of_sum(far_t, permute(far_o, other_core))
    left, right = permute(left, BLOCK_BACK[1][2]), permute(right, BLOCK_BACK[1][3])
    block_t, block_o = expert_rows(
        [[block], [permute(block, other_core)]], *weights, after=[far_t]
    )
    x, inner, *guess = kernel_call(
        forward_body,
        [like(512, part), like(512, units, dtype=jnp.float32)]
        + [like(128, part)] * 3 + [like(128, part // 2)] * 2,
        inputs, in_a, in_b, in_far, draft_in.T, draft_out,
        after=[far_t], limit=LARGE, flops=12 * 512 * part * units,
        scratch=[pltpu.VMEM((PACK * units, part), jnp.bfloat16)] * 2,
    )
    a, b = passed_on(
        [a_t, permute(a_o, other_core)], [b_t, permute(b_o, other_core)], left, right, after=[guess[0]]
    )
    guess_left, guess_right = permute(guess[3], PLANE_BACK[1][2]), permute(guess[4], PLANE_BACK[1][3])
    a, b = permute(a, BLOCK_BACK[1][0]), permute(b, BLOCK_BACK[1][1])
    block = quarters_of_sum([block_t, permute(block_o, other_core), a, b])
    guess_a, guess_b = passed_on(
        guess[1:2], guess[2:3], guess_left, guess_right, after=[block[0]]
    )
    guess_a, guess_b = permute(guess_a, PLANE_BACK[1][0]), permute(guess_b, PLANE_BACK[1][1])
    summed = pieces_of_sum(
        [block[0]] + [permute(block[i], BLOCK_BACK[0][(0, 1, 4)[i - 1]]) for i in (1, 2, 3)],
    )
    guess = quarters_of_sum([guess[0], guess_a, guess_b], after=[summed])
    guess = [guess[0]] + [permute(guess[i], PLANE_BACK[0][(0, 1, 4)[i - 1]]) for i in (3, 1, 2)]

    verified, slope = kernel_call(
        combine_body,
        [in_hbm(local_rows, width), like(32, part)],
        ids, logits, keep, hidden, *guess, exchange(summed), scratch=[wide],
    )

    slope = joined([slope, *near(slope, PLANE_RINGS[0])], order=(0, 3, 1, 2))
    slope = [slope, *near(slope, PLANE_RINGS[1])]
    other = permute(gradient(slope, x, inner, draft_out, core, 1), other_core)
    mine = gradient(slope, x, inner, draft_out, core, 0)

    def around(pieces):
        return [
            permute(pieces[k], by_core(z_step(k), z_step(-k))) if k else pieces[0] for k in Z_ORDER
        ]

    turned = kernel_call(turn_body, [like(*mine.shape[1:])] * 8, mine, other, scalars=(core, z))
    new = kernel_call(
        update_body, like(PACK * units, part // 8), *around(turned), draft_in.T, draft_out,
        scalars=(core, z),
    )
    gathered = kernel_call(
        spread_body, like(units, width), *around([new] * 8), scalars=(core, z)
    )
    other = permute(gathered, other_core)
    in_core = core[0] == 0
    new_in = jnp.where(in_core, gathered, other).T
    new_out = jnp.where(in_core, other, gathered)
    return (verified, new_in, new_out)


def solution(mesh):
    return jax.shard_map(
        per_device,
        mesh=jax.sharding.Mesh(mesh.devices.reshape(SIZES), AXES),
        in_specs=(
            P(AXES, None),
            P(AXES, None),
            P(AXES, None),
            P(AXES),
            P(None, AXES),
            P(None, AXES),
            P(AXES, None),
            P(None, PLANE),
            P(PLANE, None),
        ),
        out_specs=(P(AXES, None), P(None, PLANE), P(PLANE, None)),
        check_vma=False,
    )
```

```python
import itertools
import math

import jax
import jax.numpy as jnp
from jax import lax
from jax.experimental import pallas as pl
from jax.experimental.pallas import tpu as pltpu
from jax.sharding import PartitionSpec as P

EXPERTS = 8
DRAFT = 5
CAP = 3
LEARNING_RATE = 0.5
AXES = ("y_lo", "z_pair", "z_in", "core", "x", "y_hi")
SIZES = (2, 4, 2, 2, 4, 2)
OWNERS = ("y_lo", "z_pair")
PLANE = ("y_lo", "x", "y_hi")
PARTS = (2, 8, 2, 4, 2)


def flat(place):
    index = 0
    for size, at in zip(PARTS, place):
        index = index * size + at
    return index


def permute(value, move):
    pairs = []
    for place in itertools.product(*(range(size) for size in PARTS)):
        pairs.append((flat(place), flat(move(*place))))
    return lax.ppermute(value, AXES, pairs)


def other_core(g, z, c, x, h):
    return g, z, 1 - c, x, h


def x_step(by):
    return lambda g, z, c, x, h: (g, z, c, (x + by) % 4, h)


def y_step(by):
    def move(g, z, c, x, h):
        y = (2 * h + g + by) % 4
        return y % 2, z, c, x, y // 2

    return move


def z_step(by):
    return lambda g, z, c, x, h: (g, (z + by) % 8, c, x, h)


def z_swap(g, z, c, x, h):
    return g, z ^ 1, c, x, h


def h_swap(g, z, c, x, h):
    return g, z, c, x, 1 - h


def by_core(first, second):
    return lambda g, z, c, x, h: (second if c else first)(g, z, c, x, h)


X_RING = (x_step(1), x_step(-1), x_step(1), x_step(-1), x_step(2))
X_BACK = (x_step(-1), x_step(1), x_step(-1), x_step(1), x_step(2))
Y_RING = (y_step(1), y_step(-1), y_step(1), y_step(-1), y_step(2))
Y_BACK = (y_step(-1), y_step(1), y_step(-1), y_step(1), y_step(2))
SQUARE = (z_swap, h_swap, h_swap, z_swap, lambda g, z, c, x, h: (g, z ^ 1, c, x, 1 - h))


def mixed(first, second):
    return tuple(by_core(a, b) for a, b in zip(first, second))


BLOCK_RINGS = (mixed(SQUARE, X_RING), mixed(X_RING, SQUARE))
BLOCK_BACK = (mixed(SQUARE, X_BACK), mixed(X_BACK, SQUARE))
PLANE_RINGS = (mixed(X_RING, Y_RING), mixed(Y_RING, X_RING))
PLANE_BACK = (mixed(X_BACK, Y_BACK), mixed(Y_BACK, X_BACK))
LARGE, SMALL = 20 * 1024 * 1024, 6 * 1024 * 1024
IN_VMEM = True
Z_ORDER = (0, 2, 6, 4, 1, 7, 3, 5)
PACK = 3


def kernel_call(body, outs, *args, scalars=(), scratch=(), after=(), plain=(), hbm=0, limit=SMALL, flops=0):
    many = isinstance(outs, (list, tuple))
    listed = list(outs) if many else [outs]
    first, last = len(scalars), len(scalars) + len(args)
    idle = len(after)

    def run(*refs):
        body(*refs[:last], *refs[last + idle :])

    if IN_VMEM:
        plain = (*plain, *range(len(args) - hbm, len(args)))
        args = [
            pltpu.with_memory_space_constraint(a, pltpu.HBM if i in plain else pltpu.VMEM)
            for i, a in enumerate(args)
        ]
        after = [pltpu.with_memory_space_constraint(a, pltpu.VMEM) for a in after]
    size = sum(math.prod(a.shape) * jnp.dtype(a.dtype).itemsize for a in (*args, *listed))
    out = pl.pallas_call(
        run,
        out_shape=listed if many else outs,
        in_specs=[pl.BlockSpec(memory_space=pltpu.SMEM)] * first
        + [pl.BlockSpec(memory_space=pltpu.VMEM)] * (last - first - hbm)
        + [pl.BlockSpec(memory_space=pl.ANY)] * hbm
        + [pl.BlockSpec(memory_space=pltpu.VMEM)] * len(after),
        out_specs=[pl.BlockSpec(memory_space=pltpu.VMEM)] * len(listed)
        if many
        else pl.BlockSpec(memory_space=pltpu.VMEM),
        scratch_shapes=list(scratch),
        compiler_params=pltpu.CompilerParams(vmem_limit_bytes=limit),
        cost_estimate=pl.CostEstimate(flops=flops, bytes_accessed=size, transcendentals=0),
    )(*scalars, *args, *after)
    return out


def like(*shape, dtype=jnp.bfloat16):
    if IN_VMEM:
        return pltpu.VMEM(shape, dtype)
    return jax.ShapeDtypeStruct(shape, dtype)


def in_hbm(*shape, dtype=jnp.bfloat16):
    return jax.ShapeDtypeStruct(shape, dtype)


def dot(a, b, contract, precision=None):
    return lax.dot_general(
        a, b, (contract, ((), ())), precision=precision, preferred_element_type=jnp.float32
    )


NN, NT, TN = ((1,), (0,)), ((1,), (1,)), ((0,), (0,))


def f32(value):
    return value.astype(jnp.float32)


def near(value, ring):
    return [permute(value, ring[i]) for i in (0, 1, 4)]


def joined(pieces, after=(), order=(0, 1, 2, 3)):
    n, m = pieces[0].shape

    def body(*refs):
        for i, ref in zip(order, refs[:-1]):
            refs[-1][i * n : (i + 1) * n] = ref[...]

    return kernel_call(
        body, like(n * len(pieces), m), *[pieces[i] for i in order], after=after
    )


def halves(a, b, after=()):
    n, m = a.shape
    half = m // 2

    def body(a_ref, b_ref, left, right):
        left[...], right[...] = a_ref[:, :half], b_ref[:, half:]

    return kernel_call(body, [like(n, half)] * 2, a, b, after=after)


def halves_of_sum(a, b):
    n, m = a.shape
    half = m // 2

    def body(a_ref, b_ref, left, right):
        total = (f32(a_ref[...]) + f32(b_ref[...])).astype(jnp.bfloat16)
        left[...], right[...] = total[:, :half], total[:, half:]

    return kernel_call(body, [like(n, half)] * 2, a, b)


def passed_on(a, b, left, right, after=()):
    n, m = a[0].shape
    half, count = m // 2, len(a)

    def body(*refs):
        ins, outs = refs[: 2 * count + 2], refs[2 * count + 2 :]
        for parts, far, out, where in (
            (ins[:count], ins[-2], outs[0], slice(0, half)),
            (ins[count : 2 * count], ins[-1], outs[1], slice(half, m)),
        ):
            other = slice(half, m) if where.start == 0 else slice(0, half)
            out[:, where] = (sum(f32(p[:, where]) for p in parts) + f32(far[...])).astype(
                jnp.bfloat16
            )
            out[:, other] = sum(f32(p[:, other]) for p in parts).astype(jnp.bfloat16)

    return kernel_call(body, [like(n, m)] * 2, *a, *b, left, right, after=after)


def quarters_of_sum(parts, after=()):
    n, m = parts[0].shape
    n //= 4

    def body(*refs):
        for i, out in enumerate(refs[-4:]):
            rows = slice(i * n, (i + 1) * n)
            out[...] = sum(f32(p[rows]) for p in refs[:-4]).astype(jnp.bfloat16)

    return kernel_call(body, [like(n, m)] * 4, *parts, after=after)


def brought(value, sources, after=()):
    count = len(sources)

    def body(*refs):
        out, targets, sems = refs[count + 1], refs[count + 2 : -1], refs[-1]
        copies = [
            pltpu.make_async_copy(source, target, sems.at[i])
            for i, (source, target) in enumerate(zip(refs[1 : count + 1], targets))
        ]
        for copy in copies:
            copy.start()
        out[...] = refs[0][...]
        for copy in copies:
            copy.wait()

    return kernel_call(
        body, [like(*a.shape) for a in (value, *sources)], value, *sources, after=after,
        hbm=count, scratch=[pltpu.SemaphoreType.DMA((count,))],
    )


def rows_of(pieces, after=()):
    count, width = pieces.shape[0] * CAP, pieces.shape[2]

    def body(in_ref, out_ref, wide):
        for k in range(EXPERTS):
            wide[k * CAP : (k + 1) * CAP] = f32(in_ref[k])
        out_ref[...] = wide[...].astype(jnp.bfloat16)

    return kernel_call(
        body, like(count, width), pieces, scratch=[pltpu.VMEM((count, width), jnp.float32)],
        after=after,
    )


def pieces_of_sum(parts, after=()):
    count, width = parts[0].shape

    def body(*refs):
        ins, (out_ref, wide) = refs[:-2], refs[-2:]
        wide[...] = sum(f32(p[...]) for p in ins)
        for k in range(EXPERTS):
            out_ref[k] = wide[k * CAP : (k + 1) * CAP].astype(jnp.bfloat16)

    return kernel_call(
        body, in_hbm(EXPERTS, CAP, width), *parts, after=after,
        scratch=[pltpu.VMEM((count, width), jnp.float32)],
    )


def slots(ids, lanes):
    slot = lax.broadcasted_iota(jnp.int32, (EXPERTS * CAP, lanes), 0)
    expert, place_in = slot // CAP, slot % CAP
    named = (ids[0:1] == expert) | (ids[1:2] == expert)
    at = lax.broadcasted_iota(jnp.int32, (lanes, lanes), 0)
    to = lax.broadcasted_iota(jnp.int32, (lanes, lanes), 1)
    earlier = jnp.where((at < to) & (at // 10 == to // 10), 1.0, 0.0).astype(jnp.bfloat16)
    before = dot(jnp.where(named, 1.0, 0.0).astype(jnp.bfloat16), earlier, NN)
    return jnp.where(named & (before == f32(place_in)), 1.0, 0.0), expert


def send_body(ids_ref, hidden_ref, out_ref, wide):
    taken, _ = slots(ids_ref[...], hidden_ref.shape[0])
    wide[...] = dot(taken.astype(jnp.bfloat16), hidden_ref[...], NN)
    for k in range(EXPERTS):
        out_ref[k] = wide[k * CAP : (k + 1) * CAP].astype(jnp.bfloat16)


def pack_body(accept_ref, hidden_ref, packed_ref):
    rows, width = hidden_ref.shape
    part = width // PACK
    to = lax.broadcasted_iota(jnp.int32, (32, rows), 0)
    row = lax.broadcasted_iota(jnp.int32, (32, rows), 1)
    keep = jnp.zeros((32, rows), jnp.float32)
    for i in range(rows // DRAFT):
        kept = (row // DRAFT == i) & (row % DRAFT >= accept_ref[i])
        keep += jnp.where(kept, 1.0, 0.0)
    count = jnp.sum(keep[:1])
    total = jnp.where(lax.broadcasted_iota(jnp.int32, (32, part), 0) == 30, count, 0.0)
    for j in range(PACK):
        pick = jnp.where(to == row + 10 * j, keep, 0.0).astype(jnp.bfloat16)
        total += dot(pick, hidden_ref[:, j * part : (j + 1) * part], NN)
    packed_ref[...] = total.astype(jnp.bfloat16)


def combine_body(ids_ref, logit_ref, keep_ref, hidden_ref, *refs):
    guess, (returned_ref, verified_ref, slope_ref, wide) = refs[:4], refs[4:]
    rows, width = hidden_ref.shape
    part = width // PACK
    for k in range(EXPERTS):
        wide[k * CAP : (k + 1) * CAP] = f32(returned_ref[k])
    ids = ids_ref[...]
    taken, expert = slots(ids, 32)
    zero, one = logit_ref[0:1], logit_ref[1:2]
    first, second = 1.0 / (1.0 + jnp.exp(one - zero)), 1.0 / (1.0 + jnp.exp(zero - one))
    gated = taken * jnp.where(ids[0:1] == expert, first, second)
    combined = dot(gated[:, :rows], wide[...], TN, lax.Precision.HIGHEST)
    verified_ref[...] = (f32(hidden_ref[...]) + combined).astype(jnp.bfloat16)
    lane = lax.broadcasted_iota(jnp.int32, gated.shape, 1)
    kept = gated * keep_ref[...]
    teacher = jnp.zeros((32, part), jnp.float32)
    for j in range(PACK):
        table = jnp.where((lane >= 10 * j) & (lane < 10 * j + 10), kept, 0.0)
        teacher += dot(table, wide[:, j * part : (j + 1) * part], TN, lax.Precision.HIGHEST)
    teacher = f32(teacher.astype(jnp.bfloat16))
    slope_ref[...] = (sum(f32(g[...]) for g in guess) - teacher).astype(jnp.bfloat16)


def expert_rows(blocks, w_gate, w_up, w_down, after=()):
    width = w_gate.shape[0]
    heights = [block[0].shape[0] for block in blocks]
    flat_blocks = [part for block in blocks for part in block]
    total, count = sum(heights), len(flat_blocks)
    step = width // 6

    def body(*refs):
        ins, (gate_ref, up_ref, down_ref) = list(refs[:count]), refs[count : count + 3]
        outs, rows = refs[count + 3 : -1], refs[-1]
        at = 0
        for block, height in zip(blocks, heights):
            column = 0
            for _ in block:
                ref = ins.pop(0)
                rows[at : at + height, column : column + ref.shape[1]] = ref[...]
                column += ref.shape[1]
            at += height
        gate = dot(rows[...], gate_ref[...], NN)
        upper = dot(rows[...], up_ref[...], NN)
        acts = (gate / (1.0 + jnp.exp(-gate)) * upper).astype(jnp.bfloat16)
        for i in range(6):
            columns = slice(i * step, (i + 1) * step)
            out = dot(acts, down_ref[:, columns], NN).astype(jnp.bfloat16)
            at = 0
            for ref, height in zip(outs, heights):
                ref[:, columns] = out[at : at + height]
                at += height

    return kernel_call(
        body, [like(height, width) for height in heights], *flat_blocks, w_gate, w_up, w_down,
        scratch=[pltpu.VMEM((total, width), jnp.bfloat16)], after=after, limit=LARGE,
        flops=6 * total * width * w_gate.shape[1],
    )


def shifted(value, by):
    return pltpu.roll(value, by % value.shape[0], 0) if by else value


def fill(target, pieces):
    n = pieces[0].shape[0]
    for i, ref in enumerate(pieces):
        target[i * n : (i + 1) * n] = ref[...]


def stacked(target, source):
    units, part = source.shape[0], target.shape[1]
    for j in range(PACK):
        target[j * units : (j + 1) * units] = source[:, j * part : (j + 1) * part]


def spread_rows(value):
    return jnp.concatenate([shifted(value, 10 * j) for j in range(PACK)], axis=1).astype(
        jnp.bfloat16
    )


def gathered_rows(value, units):
    total = sum(shifted(value[:, j * units : (j + 1) * units], -10 * j) for j in range(PACK))
    row = lax.broadcasted_iota(jnp.int32, total.shape, 0) % 32
    return jnp.where(row < 10, total, 0.0)


def forward_body(*refs):
    pieces, (in_ref, out_ref), (x_ref, inner_ref, *guesses) = refs[:4], refs[4:6], refs[6:-2]
    in_rows, out_rows = refs[-2:]
    fill(x_ref, pieces)
    stacked(in_rows, in_ref)
    stacked(out_rows, out_ref)
    rows, part = x_ref.shape
    inner = gathered_rows(dot(x_ref[...], in_rows[...], NT), inner_ref.shape[1])
    inner_ref[...] = inner
    active = spread_rows(inner / (1.0 + jnp.exp(-inner)))
    guess = dot(active, out_rows[...], NN).astype(jnp.bfloat16)
    n, half = rows // 4, part // 2
    for i in range(3):
        guesses[i][...] = guess[i * n : (i + 1) * n]
    guesses[3][...], guesses[4][...] = guess[3 * n :, :half], guess[3 * n :, half:]


def put(ref, left, right):
    piece = ref.shape[2]
    grad = dot(spread_rows(left), right[...], TN).astype(jnp.bfloat16)
    for i in range(8):
        ref[i, : grad.shape[0], :] = grad[:, i * piece : (i + 1) * piece]


def gradient(pieces, x, inner, draft_out, core, of_in):
    units, part = inner.shape[1], x.shape[1]
    piece = part // 8

    def body(core_ref, *refs):
        blocks, (x_ref, inner_ref, out_ref, grad_ref, slope, out_rows) = refs[:4], refs[4:]
        fill(slope, blocks)
        inner = inner_ref[...]
        sigma = 1.0 / (1.0 + jnp.exp(-inner))
        line = lax.broadcasted_iota(jnp.int32, (x.shape[0], piece), 0) % 32
        count = jnp.sum(jnp.where(line == 30, f32(x_ref[:, :piece]), 0.0), axis=0, keepdims=True)
        high = jnp.floor(count * 0.0625)
        line = lax.broadcasted_iota(jnp.int32, (8, piece), 0)
        tail = jnp.where(line == 0, high, jnp.where(line == 1, count - 16.0 * high, 0.0))
        for i in range(8):
            grad_ref[i, PACK * units :, :] = tail.astype(jnp.bfloat16)

        @pl.when(core_ref[0] == of_in)
        def _():
            stacked(out_rows, out_ref)
            back = gathered_rows(dot(slope[...], out_rows[...], NT), units)
            put(grad_ref, back * sigma * (1.0 + inner * (1.0 - sigma)), x_ref)

        @pl.when(core_ref[0] != of_in)
        def _():
            put(grad_ref, inner * sigma, slope)

    return kernel_call(
        body, like(8, PACK * units + 8, piece), *pieces, x, inner, draft_out, scalars=(core,),
        scratch=[
            pltpu.VMEM(x.shape, jnp.bfloat16), pltpu.VMEM((PACK * units, part), jnp.bfloat16)
        ],
        plain=(5,), limit=LARGE,
    )


def place_of(z_ref, core_ref, k):
    return (z_ref[0] + 8 + k * (1 - 2 * core_ref[0])) % 8


def turn_body(core_ref, z_ref, mine_ref, other_ref, *outs):
    for k, out in enumerate(outs):
        at = place_of(z_ref, core_ref, k)
        out[...] = (f32(mine_ref[at]) + f32(other_ref[at])).astype(jnp.bfloat16)


def update_body(core_ref, z_ref, *refs):
    pieces, (in_ref, out_ref), new_ref = refs[:8], refs[8:10], refs[10]
    total = pieces[0][...].astype(jnp.float32)
    for ref in pieces[1:]:
        total += ref[...].astype(jnp.float32)
    rows, piece = new_ref.shape
    units, part = rows // PACK, in_ref.shape[1] // PACK
    rejected = 16.0 * total[rows : rows + 1] + total[rows + 1 : rows + 2]
    rate = (2.0 * LEARNING_RATE) / rejected
    in_core = jnp.full((units, piece), core_ref[0], jnp.int32) == 0
    for j in range(PACK):
        columns = pl.ds(pl.multiple_of(j * part + z_ref[0] * piece, piece), piece)
        old = jnp.where(
            in_core, in_ref[:, columns].astype(jnp.float32), out_ref[:, columns].astype(jnp.float32)
        )
        new = old - rate * total[j * units : (j + 1) * units]
        new_ref[j * units : (j + 1) * units] = new.astype(jnp.bfloat16)


def spread_body(core_ref, z_ref, *refs):
    pieces, out_ref = refs[:8], refs[8]
    rows, piece = pieces[0].shape
    units, part = rows // PACK, out_ref.shape[1] // PACK
    for k, ref in zip(Z_ORDER, pieces):
        at = place_of(z_ref, core_ref, -k)
        for j in range(PACK):
            columns = pl.ds(pl.multiple_of(j * part + at * piece, piece), piece)
            out_ref[:, columns] = ref[j * units : (j + 1) * units]


def per_device(
    hidden, expert_ids, gate_logits, accept_len, w_gate, w_up, w_down, draft_in, draft_out
):
    local_rows, width = hidden.shape
    part, units = width // PACK, draft_out.shape[0]
    core = lax.axis_index("core").astype(jnp.int32).reshape(1)
    z = (2 * lax.axis_index("z_pair") + lax.axis_index("z_in")).astype(jnp.int32).reshape(1)

    def lanes(rows, empty):
        return jnp.pad(jnp.tile(rows, (1, PACK)), ((0, 0), (0, 2)), constant_values=empty)

    keep = jnp.arange(local_rows, dtype=jnp.int32) % DRAFT >= jnp.repeat(accept_len, DRAFT)
    keep = lanes(f32(keep)[None], 0.0)
    ids = lanes(expert_ids.T, EXPERTS)
    logits = lanes(gate_logits.T, 0.0)
    wide = pltpu.VMEM((EXPERTS * CAP, width), jnp.float32)

    weights = (w_gate, w_up, w_down)
    outgoing = kernel_call(
        send_body, in_hbm(EXPERTS, CAP, width), expert_ids.T, hidden, scratch=[wide],
        plain=(0, 1), flops=2 * 24 * 10 * width,
    )
    packed = kernel_call(
        pack_body, like(32, part), hidden, scalars=(accept_len,), plain=(0,),
        flops=2 * 32 * 10 * width,
    )

    def exchange(pieces):
        return lax.all_to_all(pieces, OWNERS, split_axis=0, concat_axis=0, tiled=True)

    inputs = [packed, *near(packed, PLANE_RINGS[0])]
    own = rows_of(exchange(outgoing), after=[inputs[i] for i in (0, 3, 1, 2)])
    inputs = joined(inputs, order=(0, 3, 1, 2))
    in_a, in_b = [permute(inputs, move) for move in PLANE_RINGS[1][:2]]
    near_own = near(own, BLOCK_RINGS[0])

    block = joined([own, *near_own], after=[in_a, in_b])
    a, b = [permute(block, move) for move in BLOCK_RINGS[1][:2]]
    again, *weights = brought(inputs, weights, after=[block])
    in_far = permute(again, PLANE_RINGS[1][4])
    left, right = halves(a, b, after=[in_far])
    left, right = permute(left, BLOCK_RINGS[1][2]), permute(right, BLOCK_RINGS[1][3])
    a_t, b_t, a_o, b_o = expert_rows(
        [[a], [b], [permute(a, other_core)], [permute(b, other_core)]], *weights
    )
    far_t, far_o = expert_rows(
        [[left, right], [permute(left, other_core), permute(right, other_core)]],
        *weights, after=[a_t],
    )

    left, right = halves_of_sum(far_t, permute(far_o, other_core))
    left, right = permute(left, BLOCK_BACK[1][2]), permute(right, BLOCK_BACK[1][3])
    block_t, block_o = expert_rows(
        [[block], [permute(block, other_core)]], *weights, after=[far_t]
    )
    x, inner, *guess = kernel_call(
        forward_body,
        [like(512, part), like(512, units, dtype=jnp.float32)]
        + [like(128, part)] * 3 + [like(128, part // 2)] * 2,
        inputs, in_a, in_b, in_far, draft_in.T, draft_out,
        after=[far_t], limit=LARGE, flops=12 * 512 * part * units,
        scratch=[pltpu.VMEM((PACK * units, part), jnp.bfloat16)] * 2,
    )
    a, b = passed_on(
        [a_t, permute(a_o, other_core)], [b_t, permute(b_o, other_core)], left, right, after=[guess[0]]
    )
    guess_left, guess_right = permute(guess[3], PLANE_BACK[1][2]), permute(guess[4], PLANE_BACK[1][3])
    a, b = permute(a, BLOCK_BACK[1][0]), permute(b, BLOCK_BACK[1][1])
    block = quarters_of_sum([block_t, permute(block_o, other_core), a, b])
    guess_a, guess_b = passed_on(
        guess[1:2], guess[2:3], guess_left, guess_right, after=[block[0]]
    )
    guess_a, guess_b = permute(guess_a, PLANE_BACK[1][0]), permute(guess_b, PLANE_BACK[1][1])
    summed = pieces_of_sum(
        [block[0]] + [permute(block[i], BLOCK_BACK[0][(0, 1, 4)[i - 1]]) for i in (1, 2, 3)],
    )
    guess = quarters_of_sum([guess[0], guess_a, guess_b], after=[summed])
    guess = [guess[0]] + [permute(guess[i], PLANE_BACK[0][(0, 1, 4)[i - 1]]) for i in (3, 1, 2)]

    verified, slope = kernel_call(
        combine_body,
        [in_hbm(local_rows, width), like(32, part)],
        ids, logits, keep, hidden, *guess, exchange(summed), scratch=[wide], plain=(3, 5, 6, 7),
    )

    slope = joined([slope, *near(slope, PLANE_RINGS[0])], order=(0, 3, 1, 2))
    slope = [slope, *near(slope, PLANE_RINGS[1])]
    other = permute(gradient(slope, x, inner, draft_out, core, 1), other_core)
    mine = gradient(slope, x, inner, draft_out, core, 0)

    def around(pieces):
        return [
            permute(pieces[k], by_core(z_step(k), z_step(-k))) if k else pieces[0] for k in Z_ORDER
        ]

    turned = kernel_call(turn_body, [like(*mine.shape[1:])] * 8, mine, other, scalars=(core, z))
    new = kernel_call(
        update_body, like(PACK * units, part // 8), *around(turned), draft_in.T, draft_out,
        scalars=(core, z),
    )
    gathered = kernel_call(
        spread_body, like(units, width), *around([new] * 8), scalars=(core, z)
    )
    other = permute(gathered, other_core)
    in_core = core[0] == 0
    new_in = jnp.where(in_core, gathered, other).T
    new_out = jnp.where(in_core, other, gathered)
    return (verified, new_in, new_out)


def solution(mesh):
    return jax.shard_map(
        per_device,
        mesh=jax.sharding.Mesh(mesh.devices.reshape(SIZES), AXES),
        in_specs=(
            P(AXES, None),
            P(AXES, None),
            P(AXES, None),
            P(AXES),
            P(None, AXES),
            P(None, AXES),
            P(AXES, None),
            P(None, PLANE),
            P(PLANE, None),
        ),
        out_specs=(P(AXES, None), P(None, PLANE), P(PLANE, None)),
        check_vma=False,
    )
```
